256 devices in a mesh: col: 64 (over y, z, x_hi), rhs: 4 (over x_lo, core).
Axes of the slice: x: 4 (x_hi: 2, x_lo: 2; x = x_hi * 2 + x_lo), y: 4, z: 8, core: 2. Of those that a mesh axis runs over, the one named last changes fastest.
Arguments:
- trail_factor: bfloat16 [4096, 65536], P(None, 'col'), may hold values from -0.0234375 to 0.0234375
- trail_solution: bfloat16 [65536, 1056], P('col', 'rhs'), may hold values from -6 to 6
- window_factor: bfloat16 [4, 1024, 4096], P(None, 'col'), may hold values from -0.1875 to 0.1875
- diag_inverse: bfloat16 [4, 1024, 1024], P(None, 'col'), as said below
- right_side: float32 [4, 1024, 1056], P(None, 'col', 'rhs'), may hold values from -6 to 6
- check_weights: bfloat16 [4, 256, 32], P('rhs'), may hold values from -0.1875 to 0.1875
Outputs:
- window_solution: float32 [4, 1024, 1056], P(None, 'col', 'rhs')
- check_gap: float32 [4, 1024, 32], P(None, 'col', 'rhs')
The draws below stay inside these ranges and needn't reach their ends.
Inputs may be any that keep to these rules, and one draw needn't show every extreme that they name: Each diag_inverse[s] is upper triangular with positive diagonal.
All inputs are finite; a program needn't handle non-finite values.
Results may differ from the reference program's by a relative error of at most 0.011.
Values may be sent and summed in bfloat16 or wider, within the bound.
A program may use at most 64 MiB of HBM per device.

```python
import jax
import jax.numpy as jnp
from jax import lax

NB = 1024
WIN = 4
RHS = 1024
CHK = 32
GROUP = 256
CHKG = 8
RHSALL = 1056
N_COL = 64
N_RHS = 4


def draw_diag_inverse(key, part):
    key = jax.random.fold_in(key, 7)
    first, second = jax.random.split(key)
    base = jax.random.truncated_normal(first, -4.0, 4.0, (WIN, NB, NB), jnp.float32)
    diag_vals = jax.random.uniform(second, (WIN, NB, NB), jnp.float32, 0.5, 1.5)
    rows = lax.broadcasted_iota(jnp.int32, (WIN, NB, NB), 1)
    cols = lax.broadcasted_iota(jnp.int32, (WIN, NB, NB), 2)
    above = jnp.where(cols > rows, base * (0.7 / jnp.sqrt(jnp.float32(NB))), 0.0)
    result = above + jnp.where(cols == rows, diag_vals, 0.0)
    return result.astype(jnp.bfloat16)


def shard_levels(own_key, extent, pieces, low, top_value):
    factor_of = 1.0
    for dim, shards_of in pieces:
        draws = jax.random.uniform(jax.random.fold_in(jax.random.fold_in(own_key, 6), dim), (shards_of,), jnp.float32, low / len(pieces), top_value / len(pieces))
        factor_of = factor_of * jnp.repeat(jnp.exp(draws), extent[dim] // shards_of).reshape((-1,) + (1,) * (len(extent) - 1 - dim))
    return factor_of


def noise(key, extent, scale, reach, cuts=(), kind=jnp.bfloat16):
    array = scale * jax.random.normal(key, extent, jnp.float32)
    if cuts:
        array = array * shard_levels(key, extent, cuts, -0.22, 0.18)
    return jnp.clip(array, -reach, reach).astype(kind)


def setup_inputs(seed: int = 0) -> dict:
    key_list = jax.random.split(jax.random.key(seed), 7)
    return {
        "trail_factor": noise(key_list[0], (WIN * NB, N_COL * NB), (N_COL * NB) ** -0.5, 0.0234375, ((1, 64),)),
        "trail_solution": noise(key_list[1], (N_COL * NB, RHSALL), 1.0, 6.0, ((0, 64), (1, 4))),
        "window_factor": noise(key_list[2], (WIN, NB, WIN * NB), NB ** -0.5, 0.1875, ((1, 64),)),
        "diag_inverse": draw_diag_inverse(jax.random.fold_in(key_list[6], 71), 0),
        "right_side": noise(key_list[4], (WIN, NB, RHSALL), 1.0, 6.0, ((1, 64), (2, 4)), jnp.float32),
        "check_weights": noise(key_list[5], (N_RHS, GROUP, CHK), RHS ** -0.5, 0.1875, ((0, 4),)),
    }


def reference(trail_factor, trail_solution, window_factor, diag_inverse, right_side, check_weights):
    partial_value = jnp.dot(trail_factor, trail_solution, preferred_element_type=jnp.float32)
    partial_value = partial_value.reshape(WIN, NB, RHSALL)
    remain = [right_side[section] - partial_value[section] for section in range(WIN)]
    solved = [None] * WIN
    for section in range(WIN - 1, -1, -1):
        rounded = remain[section].astype(jnp.bfloat16)
        solved[section] = jnp.dot(diag_inverse[section], rounded, preferred_element_type=jnp.float32)
        solved_bf = solved[section].astype(jnp.bfloat16)
        for upper in range(section):
            coupling = window_factor[upper, :, section * NB:(section + 1) * NB]
            remain[upper] = remain[upper] - jnp.dot(coupling, solved_bf, preferred_element_type=jnp.float32)
    window_solution = jnp.stack(solved)
    grouped = window_solution.reshape(WIN, NB, N_RHS, GROUP + CHKG)
    rounded_all = grouped.astype(jnp.bfloat16)
    weighted = jnp.einsum("wign,gnc->wic", rounded_all[..., :GROUP].astype(jnp.float32), check_weights.astype(jnp.float32))
    weighted = weighted.reshape(WIN, NB, N_RHS, CHKG)
    check_gap = (grouped[..., GROUP:] - weighted).reshape(WIN, NB, CHK)
    return window_solution, check_gap
```

```python
import functools

import jax
import jax.numpy as jnp
from jax import lax
from jax.experimental import pallas as pl
from jax.experimental.pallas import tpu as pltpu
from jax.sharding import PartitionSpec as P

MESH = pl.DeviceIdType.MESH
BF = jnp.bfloat16
F32 = jnp.float32
NY, NZ, NX, NR = 4, 8, 2, 4
WIN = 4
NEED = [(3, 3), (2, 3), (2, 2), (1, 3), (1, 2), (1, 1), (0, 3), (0, 2), (0, 1), (0, 0)]
SLOT = {pair: i for i, pair in enumerate(NEED)}


def nt(a, b):
    return lax.dot_general(a, b, (((1,), (1,)), ((), ())), preferred_element_type=F32)


def kernel(
    f_hbm, s_ref, w_ref, d_ref, rs_ref, cw_ref, out_ref, gap_ref,
    fv, st, rs_pad, rs_t, fac,
    acc_b, acc_c, got_b1, got_c1, red_b, red_c, got_b2, got_c2, red, got3,
    rem, rg, xg, out_s, out_r, cw_pad, square, term_t, got_t,
    f_sem, fac_ss, fac_rs, fac_cs, fac_cr,
    b1_s, b1_r, c1_s, c1_r, b2_s, b2_r, c2_s, c2_r, z_s, z_r,
    rg_s, rg_r, xg_s, xg_r, o_s, o_r, t_s, t_r,
):
    col = lax.axis_index("col")
    rhs = lax.axis_index("rhs")
    y = lax.div(col, NZ * NX)
    z = lax.rem(lax.div(col, NX), NZ)
    xh = lax.rem(col, NX)
    core = lax.rem(rhs, 2)
    mine = y * NX + xh

    def at(yy, zz, xx):
        return ((yy * NZ + zz) * NX + xx, rhs)

    ypeer = [at(lax.rem(y + d, NY), z, xh) for d in range(1, NY)]
    ypos = [lax.rem(y + d, NY) for d in range(1, NY)]
    xpeer = at(y, z, 1 - xh)
    zpeer = [at(y, lax.rem(z + d, NZ), xh) for d in range(1, NZ)]
    zpos = [lax.rem(z + d, NZ) for d in range(1, NZ)]
    yxpeer = ypeer + [xpeer] + [at(lax.rem(y + d, NY), z, 1 - xh) for d in range(1, NY)]
    sibling = (col, rhs + 1 - 2 * core)
    rpeer = [(col, lax.rem(rhs + d, NR)) for d in range(1, NR)]
    rpos = [lax.rem(rhs + d, NR) for d in range(1, NR)]

    sends = []

    def send(src, dst, ss, rs, to):
        c = pltpu.make_async_remote_copy(
            src_ref=src, dst_ref=dst, send_sem=ss, recv_sem=rs, device_id=to, device_id_type=MESH
        )
        c.start()
        sends.append(c)
        return c

    for s in range(WIN - 1, -1, -1):
        for yy in range(NY):
            pltpu.make_async_copy(f_hbm.at[s, yy], fv.at[s, yy], f_sem.at[s, yy]).start()

    barrier = pltpu.get_barrier_semaphore()
    friends = yxpeer + zpeer + rpeer
    for who in friends:
        pl.semaphore_signal(barrier, inc=1, device_id=who, device_id_type=MESH)

    n = lax.broadcasted_iota(jnp.int32, (256, 256), 0)
    m = lax.broadcasted_iota(jnp.int32, (256, 256), 1)
    natural = ((m >> 4) & 7) * 32 + (m >> 7) * 16 + (m & 15)
    perm = jnp.where(n == natural, 1.0, 0.0).astype(BF)
    for g in range(NY):
        rows = []
        for r, c in NEED:
            if r == c:
                rows.append(d_ref[r, :, g * 256 : (g + 1) * 256])
            else:
                rows.append(w_ref[r, :, c * 1024 + g * 256 : c * 1024 + (g + 1) * 256])
        moved = jnp.dot(jnp.concatenate(rows, axis=0), perm, preferred_element_type=F32).astype(BF)
        moved = moved.reshape(5, 2, 16, 256)
        for a in range(5):
            for b in range(2):
                fac[a, b, z, :, g * 256 : (g + 1) * 256] = moved[a, b]

    pl.semaphore_wait(barrier, len(friends))

    right, left = zpeer[0], zpeer[-1]

    def fac_at(zz, c=None):
        return fac.at[:, core, zz]

    def fac_send(direction, step, zz, to):
        return send(fac_at(zz), fac_at(zz), fac_ss.at[direction, step], fac_rs.at[direction, step], to)

    fac_up = [fac_send(0, 0, z, right)]
    fac_down = [fac_send(1, 0, z, left)]
    shared = []

    def fac_step(step):
        if step < 4:
            zz = lax.rem(z + NZ - 1 - step, NZ)
            fac_up[step].wait_recv()
            if step < 3:
                fac_up.append(fac_send(0, step + 1, zz, right))
            shared.append(send(fac_at(zz), fac_at(zz), fac_cs.at[0, step], fac_cr.at[0, step], sibling))
        if step < 3:
            zz = lax.rem(z + 1 + step, NZ)
            fac_down[step].wait_recv()
            if step < 2:
                fac_down.append(fac_send(1, step + 1, zz, left))
            shared.append(send(fac_at(zz), fac_at(zz), fac_cs.at[1, step], fac_cr.at[1, step], sibling))

    for k in range(8):
        for c in range(2):
            piece = s_ref[k * 128 : (k + 1) * 128, c * 128 : (c + 1) * 128].astype(F32)
            st[c * 128 : (c + 1) * 128, k * 128 : (k + 1) * 128] = (-piece.T).astype(BF)
        square[...] = jnp.zeros_like(square)
        square[:, 0:8] = s_ref[k * 128 : (k + 1) * 128, 256:264].astype(F32)
        st[256:272, k * 128 : (k + 1) * 128] = (-square[...].T)[0:16].astype(BF)
    rs_pad[...] = jnp.zeros_like(rs_pad)
    for s in range(WIN):
        rs_pad[s, pl.ds(pl.multiple_of(z * 16, 16), 16), 0:264] = rs_ref[s]
        for c in range(3):
            t = rs_pad[s, :, c * 128 : (c + 1) * 128].T
            if c < 2:
                rs_t[s, c * 128 : (c + 1) * 128] = t
            else:
                rs_t[s, 256:272] = t[0:16]

    def products(s):
        def one(yy, _):
            pltpu.make_async_copy(f_hbm.at[s, yy], fv.at[s, yy], f_sem.at[s, yy]).wait()
            here = jnp.where(yy == y, 1.0, 0.0).astype(F32)
            block = jnp.concatenate(
                [fv[s, yy, :, x].reshape(128, 1024) for x in range(NX)], axis=0
            )
            both = nt(st[...], block)
            for x in range(NX):
                scale = here * jnp.where(xh == x, 1.0, 0.0).astype(F32)
                value = (both[:, x * 128 : (x + 1) * 128] + scale * rs_t[s]).astype(BF)
                acc_b[s, yy, x, 0:8] = value[0:128].reshape(8, 16, 128)
                acc_b[s, yy, x, 8:9] = value[256:272].reshape(1, 16, 128)
                acc_c[s, x, yy] = value[128:256].reshape(8, 16, 128)
            return 0

        lax.fori_loop(0, NY, one, 0)

    b1, c1, b2, c2, zz_c = {}, {}, {}, {}, {}

    def phase1_send(s):
        for d in range(NY - 1):
            b1[s, d] = send(acc_b.at[s, ypos[d]], got_b1.at[s, d], b1_s.at[s, d], b1_r.at[s, d], ypeer[d])
        c1[s] = send(acc_c.at[s, 1 - xh], got_c1.at[s], c1_s.at[s], c1_r.at[s], xpeer)

    def phase2_send(s):
        for d in range(NY - 1):
            b1[s, d].wait_recv()
        total = acc_b[s, y].astype(F32)
        for d in range(NY - 1):
            total = total + got_b1[s, d].astype(F32)
        red_b[s] = total.astype(BF)
        b2[s] = send(red_b.at[s, 1 - xh], got_b2.at[s], b2_s.at[s], b2_r.at[s], xpeer)
        c1[s].wait_recv()
        red_c[s] = (acc_c[s, xh].astype(F32) + got_c1[s].astype(F32)).astype(BF)
        for d in range(NY - 1):
            c2[s, d] = send(red_c.at[s, ypos[d]], got_c2.at[s, d], c2_s.at[s, d], c2_r.at[s, d], ypeer[d])

    def phase3_send(s):
        b2[s].wait_recv()
        total = (red_b[s, xh].astype(F32) + got_b2[s].astype(F32)).astype(BF)
        red[s, :, 0:1] = total[0:8].reshape(8, 1, 16, 128)
        for k in range(NZ):
            red[s, k, 2:3] = total[8:9]
        for d in range(NY - 1):
            c2[s, d].wait_recv()
        total = red_c[s, y].astype(F32)
        for d in range(NY - 1):
            total = total + got_c2[s, d].astype(F32)
        red[s, :, 1:2] = total.astype(BF).reshape(8, 1, 16, 128)
        for d in range(NZ - 1):
            zz_c[s, d] = send(red.at[s, zpos[d]], got3.at[s, d], z_s.at[s, d], z_r.at[s, d], zpeer[d])

    def phase3_end(s):
        for d in range(NZ - 1):
            zz_c[s, d].wait_recv()
        total = red[s, z].astype(F32)
        for d in range(NZ - 1):
            total = total + got3[s, d].astype(F32)
        rem[s] = total.reshape(48, 128)

    def gather(buf, s, value, ss, rs):
        buf[s, mine] = value
        return [
            send(buf.at[s, mine], buf.at[s, mine], ss.at[s, d], rs.at[s, d], who)
            for d, who in enumerate(yxpeer)
        ]

    def whole(buf, s):
        return jnp.concatenate([buf[s, p] for p in range(NY * NX)], axis=1)

    def factor(r, c):
        i = SLOT[r, c]
        return fac[i // 2, i % 2].reshape(128, 1024)

    outs = {}

    def out_send(s, x):
        full = jnp.concatenate([x, jnp.zeros((80, 128), F32)], axis=0).T
        out_s[s] = full.reshape(8, 16, 128)
        for d in range(NZ - 1):
            outs[s, d] = send(out_s.at[s, zpos[d]], out_r.at[s, z], o_s.at[s, d], o_r.at[s, d], zpeer[d])
        out_r[s, z] = out_s[s, z]

    lane = lax.broadcasted_iota(jnp.int32, (16, 128), 1)

    def out_end(s):
        for d in range(NZ - 1):
            outs[s, d].wait_recv()
        low = jnp.zeros((16, 128), F32)
        high = jnp.zeros((16, 128), F32)
        for k in range(NZ):
            piece = out_r[s, k]
            here = (lane >> 4) == k
            low = jnp.where(here, pltpu.roll(piece, (16 * k) % 128, 1), low)
            high = jnp.where(here, pltpu.roll(piece, (16 * k + 112) % 128, 1), high)
        out_ref[s, :, 0:128] = low
        out_ref[s, :, 128:256] = high
        out_ref[s, :, 256:264] = pltpu.roll(out_r[s, z], 96, 1)[:, 0:8]

    products(3)
    phase1_send(3)
    fac_step(0)
    products(2)
    phase1_send(2)
    phase2_send(3)
    fac_step(1)
    products(1)
    phase1_send(1)
    phase3_send(3)
    phase2_send(2)
    fac_step(2)
    products(0)
    phase1_send(0)
    phase3_end(3)
    phase3_send(2)
    phase2_send(1)
    fac_step(3)
    for c in shared:
        c.wait_recv()
    phase3_end(2)
    phase3_send(1)
    phase2_send(0)
    phase3_end(1)
    phase3_send(0)
    phase3_end(0)

    for s in range(WIN - 1, -1, -1):
        for c in gather(rg, s, rem[s].astype(BF), rg_s, rg_r):
            c.wait_recv()
        x = nt(whole(rg, s), factor(s, s))
        if s > 0:
            copies = gather(xg, s, x.astype(BF), xg_s, xg_r)
        out_send(s, x)
        if s > 0:
            for c in copies:
                c.wait_recv()
            solved = whole(xg, s)
            for r in range(s - 1, -1, -1):
                rem[r] = rem[r] - nt(solved, factor(r, s))

    for s in range(WIN - 1, -1, -1):
        out_end(s)

    cw_pad[...] = jnp.zeros_like(cw_pad)
    cw_pad[:, 0:32] = cw_ref[...]
    solved = out_ref[:, :, 0:256].reshape(64, 256).astype(BF)
    square[...] = jnp.zeros_like(square)
    square[0:64] = jnp.dot(solved, cw_pad[...], preferred_element_type=F32)
    turned = square[...].T
    term_t[...] = turned[0:32].reshape(4, 8, 128)
    ts = [
        send(term_t.at[rpos[d]], got_t.at[d], t_s.at[d], t_r.at[d], rpeer[d]) for d in range(NR - 1)
    ]
    for c in ts:
        c.wait_recv()
    total = term_t[rhs]
    for d in range(NR - 1):
        total = total + got_t[d]
    square[0:8] = total
    weighted = square[...].T
    for s in range(WIN):
        gap_ref[s] = out_ref[s, :, 256:264] - weighted[s * 16 : (s + 1) * 16, 0:8]

    for c in sends:
        c.wait_send()


def shards(trail_factor, trail_solution, window_factor, diag_inverse, right_side, check_weights):
    vm = pl.BlockSpec(memory_space=pltpu.VMEM)
    hbm = pl.BlockSpec(memory_space=pl.ANY)
    dma = pltpu.SemaphoreType.DMA
    out, gap = pl.pallas_call(
        kernel,
        out_shape=(
            jax.ShapeDtypeStruct((4, 16, 264), F32),
            jax.ShapeDtypeStruct((4, 16, 8), F32),
        ),
        in_specs=[hbm, vm, vm, vm, vm, vm],
        out_specs=(vm, vm),
        scratch_shapes=[
            pltpu.VMEM((4, 4, 8, 2, 16, 1024), BF),
            pltpu.VMEM((272, 1024), BF),
            pltpu.VMEM((4, 128, 384), F32),
            pltpu.VMEM((4, 272, 128), F32),
            pltpu.VMEM((5, 2, 8, 16, 1024), BF),
            pltpu.VMEM((4, 4, 2, 9, 16, 128), BF),
            pltpu.VMEM((4, 2, 4, 8, 16, 128), BF),
            pltpu.VMEM((4, 3, 2, 9, 16, 128), BF),
            pltpu.VMEM((4, 4, 8, 16, 128), BF),
            pltpu.VMEM((4, 2, 9, 16, 128), BF),
            pltpu.VMEM((4, 4, 8, 16, 128), BF),
            pltpu.VMEM((4, 9, 16, 128), BF),
            pltpu.VMEM((4, 3, 8, 16, 128), BF),
            pltpu.VMEM((4, 8, 3, 16, 128), BF),
            pltpu.VMEM((4, 7, 3, 16, 128), BF),
            pltpu.VMEM((4, 48, 128), F32),
            pltpu.VMEM((4, 8, 48, 128), BF),
            pltpu.VMEM((4, 8, 48, 128), BF),
            pltpu.VMEM((4, 8, 16, 128), F32),
            pltpu.VMEM((4, 8, 16, 128), F32),
            pltpu.VMEM((256, 128), BF),
            pltpu.VMEM((128, 128), F32),
            pltpu.VMEM((4, 8, 128), F32),
            pltpu.VMEM((3, 8, 128), F32),
            dma((4, 4)),
            dma((2, 4)), dma((2, 4)), dma((2, 4)), dma((2, 4)),
            dma((4, 3)), dma((4, 3)), dma((4,)), dma((4,)),
            dma((4,)), dma((4,)), dma((4, 3)), dma((4, 3)),
            dma((4, 7)), dma((4, 7)),
            dma((4, 7)), dma((4, 7)), dma((4, 7)), dma((4, 7)),
            dma((4, 7)), dma((4, 7)),
            dma((3,)), dma((3,)),
        ],
        compiler_params=pltpu.CompilerParams(
            collective_id=0, has_side_effects=True, vmem_limit_bytes=40 * 2**20
        ),
    )(
        trail_factor.reshape(4, 4, 8, 2, 16, 1024),
        trail_solution,
        window_factor,
        diag_inverse,
        right_side,
        check_weights.reshape(256, 32),
    )
    return out, gap


def solution(mesh):
    in_specs = (
        P(None, "col"),
        P("col", "rhs"),
        P(None, "col", None),
        P(None, "col", None),
        P(None, "col", "rhs"),
        P("rhs", None, None),
    )
    out_specs = (P(None, "col", "rhs"), P(None, "col", "rhs"))
    return jax.shard_map(shards, mesh=mesh, in_specs=in_specs, out_specs=out_specs, check_vma=False)
```

```python
import functools

import jax
import jax.numpy as jnp
from jax import lax
from jax.experimental import pallas as pl
from jax.experimental.pallas import tpu as pltpu
from jax.sharding import PartitionSpec as P

MESH = pl.DeviceIdType.MESH
BF = jnp.bfloat16
F32 = jnp.float32
NY, NZ, NX, NR = 4, 8, 2, 4
WIN = 4
NEED = [(3, 3), (2, 3), (2, 2), (1, 3), (1, 2), (1, 1), (0, 3), (0, 2), (0, 1), (0, 0)]
SLOT = {pair: i for i, pair in enumerate(NEED)}


def nt(a, b):
    return lax.dot_general(a, b, (((1,), (1,)), ((), ())), preferred_element_type=F32)


def kernel(
    f_hbm, s_hbm, w_hbm, d_hbm, rs_hbm, cw_hbm, out_ref, gap_ref,
    fv, st, w_ref, d_ref, rs_ref, cw_ref, rs_pad, rs_t, fac,
    acc_b, acc_c, got_b1, got_c1, red_b, red_c, got_b2, got_c2, red, got3,
    rem, rg, xg, out_s, out_r, check, term_t, got_t,
    f_sem, in_sem, fac_ss, fac_rs, fac_cs, fac_cr,
    b1_s, b1_r, c1_s, c1_r, b2_s, b2_r, c2_s, c2_r, z_s, z_r,
    rg_s, rg_r, xg_s, xg_r, o_s, o_r, t_s, t_r,
):
    col = lax.axis_index("col")
    rhs = lax.axis_index("rhs")
    y = lax.div(col, NZ * NX)
    z = lax.rem(lax.div(col, NX), NZ)
    xh = lax.rem(col, NX)
    core = lax.rem(rhs, 2)
    mine = y * NX + xh

    def at(yy, zz, xx):
        return ((yy * NZ + zz) * NX + xx, rhs)

    ypeer = [at(lax.rem(y + d, NY), z, xh) for d in range(1, NY)]
    ypos = [lax.rem(y + d, NY) for d in range(1, NY)]
    xpeer = at(y, z, 1 - xh)
    zpeer = [at(y, lax.rem(z + d, NZ), xh) for d in range(1, NZ)]
    zpos = [lax.rem(z + d, NZ) for d in range(1, NZ)]
    yxpeer = ypeer + [xpeer] + [at(lax.rem(y + d, NY), z, 1 - xh) for d in range(1, NY)]
    sibling = (col, rhs + 1 - 2 * core)
    rpeer = [(col, lax.rem(rhs + d, NR)) for d in range(1, NR)]
    rpos = [lax.rem(rhs + d, NR) for d in range(1, NR)]

    sends = []

    def send(src, dst, ss, rs, to):
        c = pltpu.make_async_remote_copy(
            src_ref=src, dst_ref=dst, send_sem=ss, recv_sem=rs, device_id=to, device_id_type=MESH
        )
        c.start()
        sends.append(c)
        return c

    s_in = pltpu.make_async_copy(s_hbm, st, in_sem.at[0])
    rs_in = pltpu.make_async_copy(rs_hbm, rs_ref, in_sem.at[1])
    d_in = pltpu.make_async_copy(d_hbm, d_ref, in_sem.at[2])
    w_in = pltpu.make_async_copy(w_hbm, w_ref, in_sem.at[3])
    cw_in = pltpu.make_async_copy(cw_hbm, cw_ref, in_sem.at[4])

    def f_start(s):
        for yy in range(NY):
            pltpu.make_async_copy(f_hbm.at[s, yy], fv.at[s, yy], f_sem.at[s, yy]).start()

    rs_in.start()
    s_in.start()
    f_start(3)
    d_in.start()
    w_in.start()
    for s in range(WIN - 2, -1, -1):
        f_start(s)
    cw_in.start()

    barrier = pltpu.get_barrier_semaphore()
    friends = yxpeer + zpeer + rpeer
    for who in friends:
        pl.semaphore_signal(barrier, inc=1, device_id=who, device_id_type=MESH)

    def permute():
        n = lax.broadcasted_iota(jnp.int32, (256, 256), 0)
        m = lax.broadcasted_iota(jnp.int32, (256, 256), 1)
        natural = ((m >> 4) & 7) * 32 + (m >> 7) * 16 + (m & 15)
        perm = jnp.where(n == natural, 1.0, 0.0).astype(BF)
        for g in range(NY):
            rows = []
            for r, c in NEED:
                if r == c:
                    rows.append(d_ref[r, :, g * 256 : (g + 1) * 256])
                else:
                    rows.append(w_ref[r, :, c * 1024 + g * 256 : c * 1024 + (g + 1) * 256])
            moved = jnp.dot(jnp.concatenate(rows, axis=0), perm, preferred_element_type=F32).astype(BF)
            moved = moved.reshape(5, 2, 16, 256)
            for a in range(5):
                for b in range(2):
                    fac[a, b, z, :, g * 256 : (g + 1) * 256] = moved[a, b]

    right, left = zpeer[0], zpeer[-1]

    def fac_at(zz, c=None):
        return fac.at[:, core, zz]

    def fac_send(direction, step, zz, to):
        return send(fac_at(zz), fac_at(zz), fac_ss.at[direction, step], fac_rs.at[direction, step], to)

    fac_up, fac_down, shared = [], [], []

    def fac_start():
        fac_up.append(fac_send(0, 0, z, right))
        fac_down.append(fac_send(1, 0, z, left))

    def fac_step(step):
        if step < 4:
            zz = lax.rem(z + NZ - 1 - step, NZ)
            fac_up[step].wait_recv()
            if step < 3:
                fac_up.append(fac_send(0, step + 1, zz, right))
            shared.append(send(fac_at(zz), fac_at(zz), fac_cs.at[0, step], fac_cr.at[0, step], sibling))
        if step < 3:
            zz = lax.rem(z + 1 + step, NZ)
            fac_down[step].wait_recv()
            if step < 2:
                fac_down.append(fac_send(1, step + 1, zz, left))
            shared.append(send(fac_at(zz), fac_at(zz), fac_cs.at[1, step], fac_cr.at[1, step], sibling))

    def turn(s):
        rs_pad[...] = jnp.zeros_like(rs_pad)
        rs_pad[pl.ds(pl.multiple_of(z * 16, 16), 16), 0:264] = rs_ref[s]
        for c in range(3):
            t = rs_pad[:, c * 128 : (c + 1) * 128].T
            if c < 2:
                rs_t[s, c * 128 : (c + 1) * 128] = t
            else:
                rs_t[s, 256:264] = t[0:8]

    def products(s):
        def one(yy, _):
            pltpu.make_async_copy(f_hbm.at[s, yy], fv.at[s, yy], f_sem.at[s, yy]).wait()
            here = jnp.where(yy == y, 1.0, 0.0).astype(F32)
            block = jnp.concatenate(
                [fv[s, yy, :, x].reshape(128, 1024) for x in range(NX)], axis=0
            )
            both = nt(st[...], block)
            for x in range(NX):
                scale = here * jnp.where(xh == x, 1.0, 0.0).astype(F32)
                value = scale * rs_t[s] - both[:, x * 128 : (x + 1) * 128]
                value = jnp.concatenate([value, jnp.zeros((8, 128), F32)], axis=0).astype(BF)
                acc_b[s, yy, x, 0:8] = value[0:128].reshape(8, 16, 128)
                acc_b[s, yy, x, 8:9] = value[256:272].reshape(1, 16, 128)
                acc_c[s, x, yy] = value[128:256].reshape(8, 16, 128)
            return 0

        lax.fori_loop(0, NY, one, 0)

    b1, c1, b2, c2, zz_c = {}, {}, {}, {}, {}

    def phase1_send(s):
        for d in range(NY - 1):
            b1[s, d] = send(acc_b.at[s, ypos[d]], got_b1.at[s, d], b1_s.at[s, d], b1_r.at[s, d], ypeer[d])
        c1[s] = send(acc_c.at[s, 1 - xh], got_c1.at[s], c1_s.at[s], c1_r.at[s], xpeer)

    def phase2_send(s):
        for d in range(NY - 1):
            b1[s, d].wait_recv()
        total = acc_b[s, y].astype(F32)
        for d in range(NY - 1):
            total = total + got_b1[s, d].astype(F32)
        red_b[s] = total.astype(BF)
        b2[s] = send(red_b.at[s, 1 - xh], got_b2.at[s], b2_s.at[s], b2_r.at[s], xpeer)
        c1[s].wait_recv()
        red_c[s] = (acc_c[s, xh].astype(F32) + got_c1[s].astype(F32)).astype(BF)
        for d in range(NY - 1):
            c2[s, d] = send(red_c.at[s, ypos[d]], got_c2.at[s, d], c2_s.at[s, d], c2_r.at[s, d], ypeer[d])

    def phase3_send(s):
        b2[s].wait_recv()
        total = (red_b[s, xh].astype(F32) + got_b2[s].astype(F32)).astype(BF)
        red[s, :, 0:1] = total[0:8].reshape(8, 1, 16, 128)
        for k in range(NZ):
            red[s, k, 2:3] = total[8:9]
        for d in range(NY - 1):
            c2[s, d].wait_recv()
        total = red_c[s, y].astype(F32)
        for d in range(NY - 1):
            total = total + got_c2[s, d].astype(F32)
        red[s, :, 1:2] = total.astype(BF).reshape(8, 1, 16, 128)
        for d in range(NZ - 1):
            zz_c[s, d] = send(red.at[s, zpos[d]], got3.at[s, d], z_s.at[s, d], z_r.at[s, d], zpeer[d])

    def phase3_end(s):
        for d in range(NZ - 1):
            zz_c[s, d].wait_recv()
        total = red[s, z].astype(F32)
        for d in range(NZ - 1):
            total = total + got3[s, d].astype(F32)
        rem[s] = rem[s] + total.reshape(48, 128)

    def gather(buf, s, value, ss, rs):
        buf[s, mine] = value
        return [
            send(buf.at[s, mine], buf.at[s, mine], ss.at[s, d], rs.at[s, d], who)
            for d, who in enumerate(yxpeer)
        ]

    def whole(buf, s):
        return jnp.concatenate([buf[s, p] for p in range(NY * NX)], axis=1)

    def factor(r, c):
        i = SLOT[r, c]
        return fac[i // 2, i % 2].reshape(128, 1024)

    outs = {}

    def out_send(s, x):
        full = jnp.concatenate([x, jnp.zeros((80, 128), F32)], axis=0).T
        out_s[s] = full.reshape(8, 16, 128)
        for d in range(NZ - 1):
            outs[s, d] = send(out_s.at[s, zpos[d]], out_r.at[s, z], o_s.at[s, d], o_r.at[s, d], zpeer[d])
        out_r[s, z] = out_s[s, z]
        check[s] = pltpu.roll(x[32:40], lax.rem(128 - 16 * z, 128), 1)

    lane = lax.broadcasted_iota(jnp.int32, (16, 128), 1)
    tcopies = {}

    def out_end(s):
        for d in range(NZ - 1):
            outs[s, d].wait_recv()
        low = jnp.zeros((16, 128), F32)
        high = jnp.zeros((16, 128), F32)
        for k in range(NZ):
            piece = out_r[s, k]
            here = (lane >> 4) == k
            low = jnp.where(here, pltpu.roll(piece, (16 * k) % 128, 1), low)
            high = jnp.where(here, pltpu.roll(piece, (16 * k + 112) % 128, 1), high)
        out_ref[s, :, 0:128] = low
        out_ref[s, :, 128:256] = high
        out_ref[s, :, 256:264] = pltpu.roll(out_r[s, z], 96, 1)[:, 0:8]

    def term_send(which):
        first, count = which[0], len(which)
        solved = out_ref[first : first + count, :, 0:256].reshape(16 * count, 256).astype(BF)
        solved = jnp.concatenate([solved, jnp.zeros((128 - 16 * count, 256), BF)], axis=0)
        term_t[first] = nt(cw_ref[...], solved).reshape(4, 8, 128)
        tcopies[first] = [
            send(term_t.at[first, rpos[d]], got_t.at[first, d], t_s.at[first, d], t_r.at[first, d], rpeer[d])
            for d in range(NR - 1)
        ]

    def term_end(which):
        first = which[0]
        for c in tcopies[first]:
            c.wait_recv()
        total = term_t[first, rhs]
        for d in range(NR - 1):
            total = total + got_t[first, d]
        for i, s in enumerate(which):
            part = total if i == 0 else pltpu.roll(total, 128 - 16 * i, 1)
            gap_ref[s] = (check[s] - part)[:, 0:16]

    rem[...] = jnp.zeros_like(rem)
    rs_in.wait()
    turn(3)
    s_in.wait()
    products(3)
    pl.semaphore_wait(barrier, len(friends))
    phase1_send(3)
    d_in.wait()
    w_in.wait()
    permute()
    fac_start()
    turn(2)
    products(2)
    phase2_send(3)
    phase1_send(2)
    turn(1)
    products(1)
    phase3_send(3)
    phase2_send(2)
    phase1_send(1)
    fac_step(0)
    turn(0)
    products(0)
    phase3_end(3)
    head = gather(rg, 3, rem[3].astype(BF), rg_s, rg_r)
    phase1_send(0)
    fac_step(1)
    phase3_send(2)
    phase2_send(1)
    fac_step(2)
    fac_step(3)
    cw_in.wait()
    for c in shared:
        c.wait_recv()

    fill = {
        ("x", 3): [(phase3_send, 1), (phase2_send, 0)],
        ("u", 3): [(phase3_end, 2)],
        ("r", 2): [(phase3_end, 1), (phase3_send, 0)],
        ("x", 2): [(phase3_end, 0)],
        ("x", 1): [(out_end, 3)],
        ("r", 0): [(out_end, 2)],
    }

    def filled(what, s):
        for f, k in fill.get((what, s), []):
            f(k)

    for s in range(WIN - 1, -1, -1):
        for c in head:
            c.wait_recv()
        x = nt(whole(rg, s), factor(s, s))
        if s > 0:
            copies = gather(xg, s, x.astype(BF), xg_s, xg_r)
        out_send(s, x)
        if s > 0:
            filled("x", s)
            for c in copies:
                c.wait_recv()
            solved = whole(xg, s)
            filled("u", s)
            rem[s - 1] = rem[s - 1] - nt(solved, factor(s - 1, s))
            head = gather(rg, s - 1, rem[s - 1].astype(BF), rg_s, rg_r)
            filled("r", s - 1)
            for r in range(s - 2, -1, -1):
                rem[r] = rem[r] - nt(solved, factor(r, s))
    out_end(1)
    term_send((1, 2, 3))
    out_end(0)
    term_send((0,))
    term_end((1, 2, 3))
    term_end((0,))

    for c in sends:
        c.wait_send()


def shards(trail_factor, trail_solution, window_factor, diag_inverse, right_side, check_weights):
    vm = pl.BlockSpec(memory_space=pltpu.VMEM)
    hbm = pl.BlockSpec(memory_space=pl.ANY)
    dma = pltpu.SemaphoreType.DMA
    out, gap = pl.pallas_call(
        kernel,
        out_shape=(
            jax.ShapeDtypeStruct((4, 16, 264), F32),
            jax.ShapeDtypeStruct((4, 8, 16), F32),
        ),
        in_specs=[hbm] * 6,
        out_specs=(vm, vm),
        scratch_shapes=[
            pltpu.VMEM((4, 4, 8, 2, 16, 1024), BF),
            pltpu.VMEM((264, 1024), BF),
            pltpu.VMEM((4, 16, 4096), BF),
            pltpu.VMEM((4, 16, 1024), BF),
            pltpu.VMEM((4, 16, 264), F32),
            pltpu.VMEM((32, 256), BF),
            pltpu.VMEM((128, 384), F32),
            pltpu.VMEM((4, 264, 128), F32),
            pltpu.VMEM((5, 2, 8, 16, 1024), BF),
            pltpu.VMEM((4, 4, 2, 9, 16, 128), BF),
            pltpu.VMEM((4, 2, 4, 8, 16, 128), BF),
            pltpu.VMEM((4, 3, 2, 9, 16, 128), BF),
            pltpu.VMEM((4, 4, 8, 16, 128), BF),
            pltpu.VMEM((4, 2, 9, 16, 128), BF),
            pltpu.VMEM((4, 4, 8, 16, 128), BF),
            pltpu.VMEM((4, 9, 16, 128), BF),
            pltpu.VMEM((4, 3, 8, 16, 128), BF),
            pltpu.VMEM((4, 8, 3, 16, 128), BF),
            pltpu.VMEM((4, 7, 3, 16, 128), BF),
            pltpu.VMEM((4, 48, 128), F32),
            pltpu.VMEM((4, 8, 48, 128), BF),
            pltpu.VMEM((4, 8, 48, 128), BF),
            pltpu.VMEM((4, 8, 16, 128), F32),
            pltpu.VMEM((4, 8, 16, 128), F32),
            pltpu.VMEM((4, 8, 128), F32),
            pltpu.VMEM((2, 4, 8, 128), F32),
            pltpu.VMEM((2, 3, 8, 128), F32),
            dma((4, 4)), dma((5,)),
            dma((2, 4)), dma((2, 4)), dma((2, 4)), dma((2, 4)),
            dma((4, 3)), dma((4, 3)), dma((4,)), dma((4,)),
            dma((4,)), dma((4,)), dma((4, 3)), dma((4, 3)),
            dma((4, 7)), dma((4, 7)),
            dma((4, 7)), dma((4, 7)), dma((4, 7)), dma((4, 7)),
            dma((4, 7)), dma((4, 7)),
            dma((2, 3)), dma((2, 3)),
        ],
        compiler_params=pltpu.CompilerParams(
            collective_id=0, has_side_effects=True, vmem_limit_bytes=60 * 2**20
        ),
    )(
        trail_factor.reshape(4, 4, 8, 2, 16, 1024),
        trail_solution.T,
        window_factor,
        diag_inverse,
        right_side,
        check_weights[0].T,
    )
    return out, gap.transpose(0, 2, 1)


def solution(mesh):
    in_specs = (
        P(None, "col"),
        P("col", "rhs"),
        P(None, "col", None),
        P(None, "col", None),
        P(None, "col", "rhs"),
        P("rhs", None, None),
    )
    out_specs = (P(None, "col", "rhs"), P(None, "col", "rhs"))
    return jax.shard_map(shards, mesh=mesh, in_specs=in_specs, out_specs=out_specs, check_vma=False)
```

```python
import functools

import jax
import jax.numpy as jnp
from jax import lax
from jax.experimental import pallas as pl
from jax.experimental.pallas import tpu as pltpu
from jax.sharding import PartitionSpec as P

MESH = pl.DeviceIdType.MESH
BF = jnp.bfloat16
F32 = jnp.float32
NY, NZ, NX, NR = 4, 8, 2, 4
WIN = 4
KEPT = [(2, 2), (1, 1), (3, 3), (0, 0), (0, 2), (0, 3)]
SLOT = {pair: i for i, pair in enumerate(KEPT)}
FOLDED = [(2, 3), (1, 2), (0, 1), (1, 3)]
FOLD = {pair: i for i, pair in enumerate(FOLDED)}


def nt(a, b):
    return lax.dot_general(a, b, (((1,), (1,)), ((), ())), preferred_element_type=F32)


def kernel(
    f_hbm, s_hbm, w_hbm, d_hbm, rs_hbm, cw_hbm, out_ref, gap_ref,
    fv, st, w_ref, d_ref, rs_ref, cw_ref, rs_pad, rs_t, fac, ws, wfull, efac,
    acc_b, acc_c, got_b1, got_c1, red_b, red_c, got_b2, got_c2, red, got3,
    rem, rg, xg, out_s, out_r, check, term_t, got_t,
    f_sem, in_sem, fac_ss, fac_rs, fac_cs, fac_cr, w1_s, w1_r, w2_s, w2_r, e_s, e_r, ec_s, ec_r,
    b1_s, b1_r, c1_s, c1_r, b2_s, b2_r, c2_s, c2_r, z_s, z_r,
    rg_s, rg_r, xg_s, xg_r, o_s, o_r, t_s, t_r,
):
    col = lax.axis_index("col")
    rhs = lax.axis_index("rhs")
    y = lax.div(col, NZ * NX)
    z = lax.rem(lax.div(col, NX), NZ)
    xh = lax.rem(col, NX)
    core = lax.rem(rhs, 2)
    mine = y * NX + xh

    def at(yy, zz, xx):
        return ((yy * NZ + zz) * NX + xx, rhs)

    ypeer = [at(lax.rem(y + d, NY), z, xh) for d in range(1, NY)]
    ypos = [lax.rem(y + d, NY) for d in range(1, NY)]
    xpeer = at(y, z, 1 - xh)
    zpeer = [at(y, lax.rem(z + d, NZ), xh) for d in range(1, NZ)]
    zpos = [lax.rem(z + d, NZ) for d in range(1, NZ)]
    yxpeer = ypeer + [xpeer] + [at(lax.rem(y + d, NY), z, 1 - xh) for d in range(1, NY)]
    sibling = (col, rhs + 1 - 2 * core)
    rpeer = [(col, lax.rem(rhs + d, NR)) for d in range(1, NR)]
    rpos = [lax.rem(rhs + d, NR) for d in range(1, NR)]

    sends = []

    def send(src, dst, ss, rs, to):
        c = pltpu.make_async_remote_copy(
            src_ref=src, dst_ref=dst, send_sem=ss, recv_sem=rs, device_id=to, device_id_type=MESH
        )
        c.start()
        sends.append(c)
        return c

    barrier = pltpu.get_barrier_semaphore()
    friends = yxpeer + zpeer + rpeer
    for who in friends:
        pl.semaphore_signal(barrier, inc=1, device_id=who, device_id_type=MESH)

    def done(copies):
        for c in copies:
            c.wait_recv()

    s_in = pltpu.make_async_copy(s_hbm, st, in_sem.at[0])
    rs_in = pltpu.make_async_copy(rs_hbm, rs_ref, in_sem.at[1])
    d_in = pltpu.make_async_copy(d_hbm, d_ref, in_sem.at[2])
    w_in = pltpu.make_async_copy(w_hbm, w_ref, in_sem.at[3])
    cw_in = pltpu.make_async_copy(cw_hbm, cw_ref, in_sem.at[4])

    def f_start(s):
        for yy in range(NY):
            pltpu.make_async_copy(f_hbm.at[s, yy], fv.at[s, yy], f_sem.at[s, yy]).start()

    rs_in.start()
    s_in.start()
    f_start(3)
    d_in.start()
    w_in.start()
    for s in range(WIN - 2, -1, -1):
        f_start(s)
    cw_in.start()

    def permute():
        n = lax.broadcasted_iota(jnp.int32, (256, 256), 0)
        m = lax.broadcasted_iota(jnp.int32, (256, 256), 1)
        natural = ((m >> 4) & 7) * 32 + (m >> 7) * 16 + (m & 15)
        perm = jnp.where(n == natural, 1.0, 0.0).astype(BF)
        for g in range(NY):
            rows = []
            for r, c in KEPT + FOLDED:
                if r == c:
                    rows.append(d_ref[r, :, g * 256 : (g + 1) * 256])
                else:
                    rows.append(w_ref[r, :, c * 1024 + g * 256 : c * 1024 + (g + 1) * 256])
            moved = jnp.dot(jnp.concatenate(rows, axis=0), perm, preferred_element_type=F32).astype(BF)
            moved = moved.reshape(10, 16, 256)
            for a in range(3):
                fac[a, core, z, :, g * 256 : (g + 1) * 256] = jnp.where(core == 0, moved[2 * a], moved[2 * a + 1])
            for i in range(4):
                for x in range(NX):
                    ws[i // 2, i % 2, g * NX + x] = moved[6 + i, :, x * 128 : (x + 1) * 128]

    fac_c, fac_shared, e_c, e_shared, w1, w2 = {}, {}, {}, {}, [], {}

    def fac_send(a):
        part = fac.at[a, core, z]
        fac_c[a] = [send(part, part, fac_ss.at[a, d], fac_rs.at[a, d], zpeer[d]) for d in range(NZ - 1)]

    def ring_send(a, direction, step, zz):
        part = fac.at[a, core, zz]
        to = zpeer[-1] if direction else zpeer[0]
        slot = 4 * direction + step
        return send(part, part, fac_ss.at[a, slot], fac_rs.at[a, slot], to)

    ups, downs = {}, {}

    def ring_start(a):
        ups[a] = [ring_send(a, 0, 0, z)]
        downs[a] = [ring_send(a, 1, 0, z)]
        fac_c[a] = []

    def ring_step(a, step):
        ups[a][step].wait_recv()
        if step < 3:
            ups[a].append(ring_send(a, 0, step + 1, lax.rem(z + NZ - 1 - step, NZ)))
            downs[a][step].wait_recv()
            if step < 2:
                downs[a].append(ring_send(a, 1, step + 1, lax.rem(z + 1 + step, NZ)))

    def fac_share(a):
        done(fac_c[a])
        fac_shared[a] = send(fac.at[a, core], fac.at[a, core], fac_cs.at[a], fac_cr.at[a], sibling)

    def fac_end(a):
        fac_shared[a].wait_recv()

    def w1_send():
        wfull[mine, :, z] = ws[:, core, z]
        for d in range(NZ - 1):
            w1.append(send(ws.at[:, core, zpos[d]], wfull.at[mine, :, z], w1_s.at[d], w1_r.at[d], zpeer[d]))

    def w2_send(i):
        if i == 0:
            done(w1)
        part = wfull.at[mine, i]
        w2[i] = [send(part, part, w2_s.at[i, d], w2_r.at[i, d], who) for d, who in enumerate(yxpeer)]

    def e_send(i):
        done(w2[i])
        inverse = (fac[0, core] if i == 0 else fac[1 - core, 1]).reshape(128, 1024)
        block = jnp.concatenate([wfull[p, i].reshape(128, 128) for p in range(NY * NX)], axis=0)
        efac[i, core, z] = jnp.dot(inverse, block, preferred_element_type=F32).astype(BF)
        part = efac.at[i, core, z]
        e_c[i] = [send(part, part, e_s.at[i, d], e_r.at[i, d], zpeer[d]) for d in range(NZ - 1)]

    def e_share(i):
        done(e_c[i])
        e_shared[i] = send(efac.at[i, core], efac.at[i, core], ec_s.at[i], ec_r.at[i], sibling)

    def e_end(i):
        e_shared[i].wait_recv()

    def folded(r, c):
        i = FOLD[r, c]
        return jnp.concatenate([efac[i // 2, i % 2, k] for k in range(NZ)], axis=1)

    def turn(s):
        rs_pad[...] = jnp.zeros_like(rs_pad)
        rs_pad[pl.ds(pl.multiple_of(z * 16, 16), 16), 0:264] = rs_ref[s]
        for c in range(3):
            t = rs_pad[:, c * 128 : (c + 1) * 128].T
            if c < 2:
                rs_t[s, c * 128 : (c + 1) * 128] = t
            else:
                rs_t[s, 256:264] = t[0:8]

    def products(s):
        def one(yy, _):
            pltpu.make_async_copy(f_hbm.at[s, yy], fv.at[s, yy], f_sem.at[s, yy]).wait()
            here = jnp.where(yy == y, 1.0, 0.0).astype(F32)
            block = jnp.concatenate(
                [fv[s, yy, :, x].reshape(128, 1024) for x in range(NX)], axis=0
            )
            both = nt(st[...], block)
            for x in range(NX):
                scale = here * jnp.where(xh == x, 1.0, 0.0).astype(F32)
                value = scale * rs_t[s] - both[:, x * 128 : (x + 1) * 128]
                value = jnp.concatenate([value, jnp.zeros((8, 128), F32)], axis=0).astype(BF)
                acc_b[s, yy, x, 0:8] = value[0:128].reshape(8, 16, 128)
                acc_b[s, yy, x, 8:9] = value[256:272].reshape(1, 16, 128)
                acc_c[s, x, yy] = value[128:256].reshape(8, 16, 128)
            return 0

        lax.fori_loop(0, NY, one, 0)

    b1, c1, b2, c2, zz_c = {}, {}, {}, {}, {}

    def phase1_send(s):
        for d in range(NY - 1):
            b1[s, d] = send(acc_b.at[s, ypos[d]], got_b1.at[s, d], b1_s.at[s, d], b1_r.at[s, d], ypeer[d])
        c1[s] = send(acc_c.at[s, 1 - xh], got_c1.at[s], c1_s.at[s], c1_r.at[s], xpeer)

    def phase2_send(s):
        for d in range(NY - 1):
            b1[s, d].wait_recv()
        total = acc_b[s, y].astype(F32)
        for d in range(NY - 1):
            total = total + got_b1[s, d].astype(F32)
        red_b[s] = total.astype(BF)
        b2[s] = send(red_b.at[s, 1 - xh], got_b2.at[s], b2_s.at[s], b2_r.at[s], xpeer)
        c1[s].wait_recv()
        red_c[s] = (acc_c[s, xh].astype(F32) + got_c1[s].astype(F32)).astype(BF)
        for d in range(NY - 1):
            c2[s, d] = send(red_c.at[s, ypos[d]], got_c2.at[s, d], c2_s.at[s, d], c2_r.at[s, d], ypeer[d])

    def phase3_send(s):
        b2[s].wait_recv()
        total = (red_b[s, xh].astype(F32) + got_b2[s].astype(F32)).astype(BF)
        red[s, :, 0:1] = total[0:8].reshape(8, 1, 16, 128)
        for k in range(NZ):
            red[s, k, 2:3] = total[8:9]
        for d in range(NY - 1):
            c2[s, d].wait_recv()
        total = red_c[s, y].astype(F32)
        for d in range(NY - 1):
            total = total + got_c2[s, d].astype(F32)
        red[s, :, 1:2] = total.astype(BF).reshape(8, 1, 16, 128)
        for d in range(NZ - 1):
            zz_c[s, d] = send(red.at[s, zpos[d]], got3.at[s, d], z_s.at[s, d], z_r.at[s, d], zpeer[d])

    def phase3_end(s):
        for d in range(NZ - 1):
            zz_c[s, d].wait_recv()
        total = red[s, z].astype(F32)
        for d in range(NZ - 1):
            total = total + got3[s, d].astype(F32)
        rem[s] = rem[s] + total.reshape(48, 128)

    def gather(buf, s, value, ss, rs):
        buf[s, mine] = value
        return [
            send(buf.at[s, mine], buf.at[s, mine], ss.at[s, d], rs.at[s, d], who)
            for d, who in enumerate(yxpeer)
        ]

    def whole(buf, s):
        return jnp.concatenate([buf[s, p] for p in range(NY * NX)], axis=1)

    def factor(r, c):
        i = SLOT[r, c]
        return fac[i // 2, i % 2].reshape(128, 1024)

    outs = {}

    def out_send(s, x):
        full = jnp.concatenate([x, jnp.zeros((80, 128), F32)], axis=0).T
        out_s[s] = full.reshape(8, 16, 128).astype(BF)
        for d in range(NZ - 1):
            outs[s, d] = send(out_s.at[s, zpos[d]], out_r.at[s, z], o_s.at[s, d], o_r.at[s, d], zpeer[d])
        out_r[s, z] = out_s[s, z]
        check[s] = pltpu.roll(x[32:40], lax.rem(128 - 16 * z, 128), 1)

    lane = lax.broadcasted_iota(jnp.int32, (16, 128), 1)
    tcopies = {}

    def out_end(s):
        for d in range(NZ - 1):
            outs[s, d].wait_recv()
        low = jnp.zeros((16, 128), F32)
        high = jnp.zeros((16, 128), F32)
        for k in range(NZ):
            piece = out_r[s, k].astype(F32)
            here = (lane >> 4) == k
            low = jnp.where(here, pltpu.roll(piece, (16 * k) % 128, 1), low)
            high = jnp.where(here, pltpu.roll(piece, (16 * k + 112) % 128, 1), high)
        out_ref[s, :, 0:128] = low
        out_ref[s, :, 128:256] = high
        out_ref[s, :, 256:264] = pltpu.roll(out_r[s, z].astype(F32), 96, 1)[:, 0:8]

    def term_send(which):
        first, count = which[0], len(which)
        solved = out_ref[first : first + count, :, 0:256].reshape(16 * count, 256).astype(BF)
        solved = jnp.concatenate([solved, jnp.zeros((128 - 16 * count, 256), BF)], axis=0)
        term_t[first] = nt(cw_ref[...], solved).reshape(4, 8, 128)
        tcopies[first] = [
            send(term_t.at[first, rpos[d]], got_t.at[first, d], t_s.at[first, d], t_r.at[first, d], rpeer[d])
            for d in range(NR - 1)
        ]

    def term_end(which):
        first = which[0]
        for c in tcopies[first]:
            c.wait_recv()
        total = term_t[first, rhs]
        for d in range(NR - 1):
            total = total + got_t[first, d]
        for i, s in enumerate(which):
            part = total if i == 0 else pltpu.roll(total, 128 - 16 * i, 1)
            gap_ref[s] = (check[s] - part)[:, 0:16]

    rem[...] = jnp.zeros_like(rem)
    rs_in.wait()
    turn(3)
    s_in.wait()
    products(3)
    d_in.wait()
    w_in.wait()
    permute()
    pl.semaphore_wait(barrier, len(friends))
    phase1_send(3)
    w1_send()
    fac_send(0)
    turn(2)
    products(2)
    w2_send(0)
    phase2_send(3)
    w2_send(1)
    fac_send(1)
    phase1_send(2)
    turn(1)
    products(1)
    fac_share(0)
    phase3_send(3)
    e_send(0)
    turn(0)
    products(0)
    fac_share(1)
    phase2_send(2)
    phase1_send(1)
    phase3_end(3)
    head = gather(rg, 3, rem[3].astype(BF), rg_s, rg_r)
    fac_end(1)
    e_send(1)
    phase3_send(2)
    phase2_send(1)
    phase1_send(0)

    done(head)
    x = nt(whole(rg, 3), factor(3, 3))
    copies = gather(xg, 3, x.astype(BF), xg_s, xg_r)
    out_send(3, x)
    e_share(0)
    phase3_end(2)
    head = gather(rg, 2, rem[2].astype(BF), rg_s, rg_r)
    phase3_send(1)
    phase2_send(0)
    fac_send(2)
    fac_end(0)
    done(head)
    x = nt(whole(rg, 2), factor(2, 2))
    done(copies)
    e_end(0)
    x = x - nt(whole(xg, 3), folded(2, 3))
    copies = gather(xg, 2, x.astype(BF), xg_s, xg_r)
    out_send(2, x)

    phase3_end(1)
    head = gather(rg, 1, rem[1].astype(BF), rg_s, rg_r)
    phase3_send(0)
    e_share(1)
    fac_share(2)
    done(head)
    e_end(1)
    x = nt(whole(rg, 1), factor(1, 1)) - nt(whole(xg, 3), folded(1, 3))
    done(copies)
    x = x - nt(whole(xg, 2), folded(1, 2))
    copies = gather(xg, 1, x.astype(BF), xg_s, xg_r)
    phase3_end(0)
    fac_end(2)
    rem[0] = rem[0] - nt(whole(xg, 3), factor(0, 3)) - nt(whole(xg, 2), factor(0, 2))
    head = gather(rg, 0, rem[0].astype(BF), rg_s, rg_r)
    out_send(1, x)
    out_end(3)
    cw_in.wait()
    done(head)
    x = nt(whole(rg, 0), factor(0, 0))
    done(copies)
    x = x - nt(whole(xg, 1), folded(0, 1))
    out_send(0, x)
    out_end(2)
    out_end(1)
    term_send((1, 2, 3))
    out_end(0)
    term_send((0,))
    term_end((1, 2, 3))
    term_end((0,))

    for c in sends:
        c.wait_send()


def shards(trail_factor, trail_solution, window_factor, diag_inverse, right_side, check_weights):
    vm = pl.BlockSpec(memory_space=pltpu.VMEM)
    hbm = pl.BlockSpec(memory_space=pl.ANY)
    dma = pltpu.SemaphoreType.DMA
    out, gap = pl.pallas_call(
        kernel,
        out_shape=(
            jax.ShapeDtypeStruct((4, 16, 264), F32),
            jax.ShapeDtypeStruct((4, 8, 16), F32),
        ),
        in_specs=[hbm] * 6,
        out_specs=(vm, vm),
        scratch_shapes=[
            pltpu.VMEM((4, 4, 8, 2, 16, 1024), BF),
            pltpu.VMEM((264, 1024), BF),
            pltpu.VMEM((4, 16, 4096), BF),
            pltpu.VMEM((4, 16, 1024), BF),
            pltpu.VMEM((4, 16, 264), F32),
            pltpu.VMEM((32, 256), BF),
            pltpu.VMEM((128, 384), F32),
            pltpu.VMEM((4, 264, 128), F32),
            pltpu.VMEM((3, 2, 8, 16, 1024), BF),
            pltpu.VMEM((2, 2, 8, 16, 128), BF),
            pltpu.VMEM((8, 2, 8, 16, 128), BF),
            pltpu.VMEM((2, 2, 8, 128, 128), BF),
            pltpu.VMEM((4, 4, 2, 9, 16, 128), BF),
            pltpu.VMEM((4, 2, 4, 8, 16, 128), BF),
            pltpu.VMEM((4, 3, 2, 9, 16, 128), BF),
            pltpu.VMEM((4, 4, 8, 16, 128), BF),
            pltpu.VMEM((4, 2, 9, 16, 128), BF),
            pltpu.VMEM((4, 4, 8, 16, 128), BF),
            pltpu.VMEM((4, 9, 16, 128), BF),
            pltpu.VMEM((4, 3, 8, 16, 128), BF),
            pltpu.VMEM((4, 8, 3, 16, 128), BF),
            pltpu.VMEM((4, 7, 3, 16, 128), BF),
            pltpu.VMEM((4, 48, 128), F32),
            pltpu.VMEM((4, 8, 48, 128), BF),
            pltpu.VMEM((4, 8, 48, 128), BF),
            pltpu.VMEM((4, 8, 16, 128), BF),
            pltpu.VMEM((4, 8, 16, 128), BF),
            pltpu.VMEM((4, 8, 128), F32),
            pltpu.VMEM((2, 4, 8, 128), F32),
            pltpu.VMEM((2, 3, 8, 128), F32),
            dma((4, 4)), dma((5,)),
            dma((3, 8)), dma((3, 8)), dma((3,)), dma((3,)),
            dma((7,)), dma((7,)), dma((2, 7)), dma((2, 7)), dma((2, 7)), dma((2, 7)), dma((2,)), dma((2,)),
            dma((4, 3)), dma((4, 3)), dma((4,)), dma((4,)),
            dma((4,)), dma((4,)), dma((4, 3)), dma((4, 3)),
            dma((4, 7)), dma((4, 7)),
            dma((4, 7)), dma((4, 7)), dma((4, 7)), dma((4, 7)),
            dma((4, 7)), dma((4, 7)),
            dma((2, 3)), dma((2, 3)),
        ],
        compiler_params=pltpu.CompilerParams(
            collective_id=0, has_side_effects=True, vmem_limit_bytes=60 * 2**20
        ),
    )(
        trail_factor.reshape(4, 4, 8, 2, 16, 1024),
        trail_solution.T,
        window_factor,
        diag_inverse,
        right_side,
        check_weights[0].T,
    )
    return out, gap.transpose(0, 2, 1)


def solution(mesh):
    in_specs = (
        P(None, "col"),
        P("col", "rhs"),
        P(None, "col", None),
        P(None, "col", None),
        P(None, "col", "rhs"),
        P("rhs", None, None),
    )
    out_specs = (P(None, "col", "rhs"), P(None, "col", "rhs"))
    return jax.shard_map(shards, mesh=mesh, in_specs=in_specs, out_specs=out_specs, check_vma=False)
```

```python
import functools

import jax
import jax.numpy as jnp
from jax import lax
from jax.experimental import pallas as pl
from jax.experimental.pallas import tpu as pltpu
from jax.sharding import PartitionSpec as P

MESH = pl.DeviceIdType.MESH
BF = jnp.bfloat16
F32 = jnp.float32
NY, NZ, NX, NR = 4, 8, 2, 4
WIN = 4
KEPT = [(2, 2), (1, 1), (3, 3), (0, 0), (0, 2), (0, 3)]
SLOT = {pair: i for i, pair in enumerate(KEPT)}
FOLDED = [(2, 3), (1, 2), (0, 1), (1, 3)]
FOLD = {pair: i for i, pair in enumerate(FOLDED)}


def nt(a, b):
    return lax.dot_general(a, b, (((1,), (1,)), ((), ())), preferred_element_type=F32)


def kernel(
    f_hbm, s_hbm, w_hbm, d_hbm, rs_hbm, cw_hbm, out_ref, gap_ref,
    fv, st, w_ref, d_ref, rs_ref, cw_ref, rs_pad, rs_t, fac, ws, wfull, efac,
    acc_b, acc_c, got_b1, got_c1, red_b, red_c, got_b2, got_c2, red, got3,
    rem, rg, xg, out_s, out_r, check, term_t, got_t,
    f_sem, in_sem, fac_ss, fac_rs, fac_cs, fac_cr, w1_s, w1_r, w2_s, w2_r, e_s, e_r, ec_s, ec_r,
    b1_s, b1_r, c1_s, c1_r, b2_s, b2_r, c2_s, c2_r, z_s, z_r,
    rg_s, rg_r, xg_s, xg_r, o_s, o_r, t_s, t_r,
):
    col = lax.axis_index("col")
    rhs = lax.axis_index("rhs")
    y = lax.div(col, NZ * NX)
    z = lax.rem(lax.div(col, NX), NZ)
    xh = lax.rem(col, NX)
    core = lax.rem(rhs, 2)
    mine = y * NX + xh

    def at(yy, zz, xx):
        return ((yy * NZ + zz) * NX + xx, rhs)

    ypeer = [at(lax.rem(y + d, NY), z, xh) for d in range(1, NY)]
    ypos = [lax.rem(y + d, NY) for d in range(1, NY)]
    xpeer = at(y, z, 1 - xh)
    zpeer = [at(y, lax.rem(z + d, NZ), xh) for d in range(1, NZ)]
    zpos = [lax.rem(z + d, NZ) for d in range(1, NZ)]
    yxpeer = ypeer + [xpeer] + [at(lax.rem(y + d, NY), z, 1 - xh) for d in range(1, NY)]
    sibling = (col, rhs + 1 - 2 * core)
    rpeer = [(col, lax.rem(rhs + d, NR)) for d in range(1, NR)]
    rpos = [lax.rem(rhs + d, NR) for d in range(1, NR)]

    sends = []

    def send(src, dst, ss, rs, to):
        c = pltpu.make_async_remote_copy(
            src_ref=src, dst_ref=dst, send_sem=ss, recv_sem=rs, device_id=to, device_id_type=MESH
        )
        c.start()
        sends.append(c)
        return c

    barrier = pltpu.get_barrier_semaphore()
    friends = yxpeer + zpeer + rpeer
    for who in friends:
        pl.semaphore_signal(barrier, inc=1, device_id=who, device_id_type=MESH)

    def done(copies):
        for c in copies:
            c.wait_recv()

    s_in = pltpu.make_async_copy(s_hbm, st, in_sem.at[0])
    rs_in = pltpu.make_async_copy(rs_hbm, rs_ref, in_sem.at[1])
    d_in = pltpu.make_async_copy(d_hbm, d_ref, in_sem.at[2])
    w_in = pltpu.make_async_copy(w_hbm, w_ref, in_sem.at[3])
    cw_in = pltpu.make_async_copy(cw_hbm, cw_ref, in_sem.at[4])

    def f_start(s):
        for yy in range(NY):
            pltpu.make_async_copy(f_hbm.at[s, yy], fv.at[s, yy], f_sem.at[s, yy]).start()

    rs_in.start()
    s_in.start()
    f_start(3)
    d_in.start()
    w_in.start()
    for s in range(WIN - 2, -1, -1):
        f_start(s)
    cw_in.start()

    def permute():
        n = lax.broadcasted_iota(jnp.int32, (256, 256), 0)
        m = lax.broadcasted_iota(jnp.int32, (256, 256), 1)
        natural = ((m >> 4) & 7) * 32 + (m >> 7) * 16 + (m & 15)
        perm = jnp.where(n == natural, 1.0, 0.0).astype(BF)
        for g in range(NY):
            rows = []
            for r, c in KEPT + FOLDED:
                if r == c:
                    rows.append(d_ref[r, :, g * 256 : (g + 1) * 256])
                else:
                    rows.append(w_ref[r, :, c * 1024 + g * 256 : c * 1024 + (g + 1) * 256])
            moved = jnp.dot(jnp.concatenate(rows, axis=0), perm, preferred_element_type=F32).astype(BF)
            moved = moved.reshape(10, 16, 256)
            for a in range(3):
                fac[a, core, z, :, g * 256 : (g + 1) * 256] = jnp.where(core == 0, moved[2 * a], moved[2 * a + 1])
            for i in range(4):
                for x in range(NX):
                    ws[i // 2, i % 2, g * NX + x] = moved[6 + i, :, x * 128 : (x + 1) * 128]

    fac_c, fac_shared, e_c, e_shared, w1, w2 = {}, {}, {}, {}, [], {}

    def fac_send(a):
        part = fac.at[a, core, z]
        fac_c[a] = [send(part, part, fac_ss.at[a, d], fac_rs.at[a, d], zpeer[d]) for d in range(NZ - 1)]

    def ring_send(a, direction, step, zz):
        part = fac.at[a, core, zz]
        to = zpeer[-1] if direction else zpeer[0]
        slot = 4 * direction + step
        return send(part, part, fac_ss.at[a, slot], fac_rs.at[a, slot], to)

    ups, downs = {}, {}

    def ring_start(a):
        ups[a] = [ring_send(a, 0, 0, z)]
        downs[a] = [ring_send(a, 1, 0, z)]
        fac_c[a] = []

    def ring_step(a, step):
        ups[a][step].wait_recv()
        if step < 3:
            ups[a].append(ring_send(a, 0, step + 1, lax.rem(z + NZ - 1 - step, NZ)))
            downs[a][step].wait_recv()
            if step < 2:
                downs[a].append(ring_send(a, 1, step + 1, lax.rem(z + 1 + step, NZ)))

    def fac_share(a):
        done(fac_c[a])
        fac_shared[a] = send(fac.at[a, core], fac.at[a, core], fac_cs.at[a], fac_cr.at[a], sibling)

    def fac_end(a):
        fac_shared[a].wait_recv()

    def w1_send():
        wfull[mine, :, z] = ws[:, core, z]
        for d in range(NZ - 1):
            w1.append(send(ws.at[:, core, zpos[d]], wfull.at[mine, :, z], w1_s.at[d], w1_r.at[d], zpeer[d]))

    def w2_send(i):
        if i == 0:
            done(w1)
        part = wfull.at[mine, i]
        w2[i] = [send(part, part, w2_s.at[i, d], w2_r.at[i, d], who) for d, who in enumerate(yxpeer)]

    def e_send(i):
        done(w2[i])
        inverse = (fac[0, core] if i == 0 else fac[1 - core, 1]).reshape(128, 1024)
        block = jnp.concatenate([wfull[p, i].reshape(128, 128) for p in range(NY * NX)], axis=0)
        efac[i, core, z] = jnp.dot(inverse, block, preferred_element_type=F32).astype(BF)
        part = efac.at[i, core, z]
        e_c[i] = [send(part, part, e_s.at[i, d], e_r.at[i, d], zpeer[d]) for d in range(NZ - 1)]

    def e_share(i):
        done(e_c[i])
        e_shared[i] = send(efac.at[i, core], efac.at[i, core], ec_s.at[i], ec_r.at[i], sibling)

    def e_end(i):
        e_shared[i].wait_recv()

    def folded(r, c):
        i = FOLD[r, c]
        return jnp.concatenate([efac[i // 2, i % 2, k] for k in range(NZ)], axis=1)

    def turn(s):
        rs_pad[...] = jnp.zeros_like(rs_pad)
        rs_pad[pl.ds(pl.multiple_of(z * 16, 16), 16), 0:264] = rs_ref[s]
        for c in range(3):
            t = rs_pad[:, c * 128 : (c + 1) * 128].T
            if c < 2:
                rs_t[s, c * 128 : (c + 1) * 128] = t
            else:
                rs_t[s, 256:264] = t[0:8]

    def products(s):
        def one(yy, _):
            pltpu.make_async_copy(f_hbm.at[s, yy], fv.at[s, yy], f_sem.at[s, yy]).wait()
            here = jnp.where(yy == y, 1.0, 0.0).astype(F32)
            block = jnp.concatenate(
                [fv[s, yy, :, x].reshape(128, 1024) for x in range(NX)], axis=0
            )
            both = nt(st[...], block)
            for x in range(NX):
                scale = here * jnp.where(xh == x, 1.0, 0.0).astype(F32)
                value = scale * rs_t[s] - both[:, x * 128 : (x + 1) * 128]
                value = jnp.concatenate([value, jnp.zeros((8, 128), F32)], axis=0).astype(BF)
                acc_b[s, yy, x, 0:8] = value[0:128].reshape(8, 16, 128)
                acc_b[s, yy, x, 8:9] = value[256:272].reshape(1, 16, 128)
                acc_c[s, x, yy] = value[128:256].reshape(8, 16, 128)
            return 0

        lax.fori_loop(0, NY, one, 0)

    b1, c1, b2, c2, zz_c = {}, {}, {}, {}, {}

    def phase1_send(s, n=1):
        g = pl.ds(s, n)
        for d in range(NY - 1):
            b1[s, d] = send(acc_b.at[g, ypos[d]], got_b1.at[g, d], b1_s.at[s, d], b1_r.at[s, d], ypeer[d])
        c1[s] = send(acc_c.at[g, 1 - xh], got_c1.at[g], c1_s.at[s], c1_r.at[s], xpeer)

    def phase2_send(s, n=1):
        g = pl.ds(s, n)
        for d in range(NY - 1):
            b1[s, d].wait_recv()
        total = acc_b[g, y].astype(F32)
        for d in range(NY - 1):
            total = total + got_b1[g, d].astype(F32)
        red_b[g] = total.astype(BF)
        b2[s] = send(red_b.at[g, 1 - xh], got_b2.at[g], b2_s.at[s], b2_r.at[s], xpeer)
        c1[s].wait_recv()
        red_c[g] = (acc_c[g, xh].astype(F32) + got_c1[g].astype(F32)).astype(BF)
        for d in range(NY - 1):
            c2[s, d] = send(red_c.at[g, ypos[d]], got_c2.at[g, d], c2_s.at[s, d], c2_r.at[s, d], ypeer[d])

    def phase3_send(s, n=1):
        g = pl.ds(s, n)
        b2[s].wait_recv()
        total = (red_b[g, xh].astype(F32) + got_b2[g].astype(F32)).astype(BF)
        for i in range(n):
            red[s + i, :, 0:1] = total[i, 0:8].reshape(8, 1, 16, 128)
            for k in range(NZ):
                red[s + i, k, 2:3] = total[i, 8:9]
        for d in range(NY - 1):
            c2[s, d].wait_recv()
        total = red_c[g, y].astype(F32)
        for d in range(NY - 1):
            total = total + got_c2[g, d].astype(F32)
        total = total.astype(BF)
        for i in range(n):
            red[s + i, :, 1:2] = total[i].reshape(8, 1, 16, 128)
        for d in range(NZ - 1):
            zz_c[s, d] = send(red.at[g, zpos[d]], got3.at[g, d], z_s.at[s, d], z_r.at[s, d], zpeer[d])

    def phase3_end(s, n=1):
        for d in range(NZ - 1):
            zz_c[s, d].wait_recv()
        for i in range(s, s + n):
            total = red[i, z].astype(F32)
            for d in range(NZ - 1):
                total = total + got3[i, d].astype(F32)
            rem[i] = total.reshape(48, 128)

    def gather(buf, s, value, ss, rs):
        buf[s, mine] = value
        return [
            send(buf.at[s, mine], buf.at[s, mine], ss.at[s, d], rs.at[s, d], who)
            for d, who in enumerate(yxpeer)
        ]

    def whole(buf, s):
        return jnp.concatenate([buf[s, p] for p in range(NY * NX)], axis=1)

    def factor(r, c):
        i = SLOT[r, c]
        return fac[i // 2, i % 2].reshape(128, 1024)

    outs = {}

    def out_keep(s, x):
        full = jnp.concatenate([x, jnp.zeros((80, 128), F32)], axis=0).T
        out_s[s] = full.reshape(8, 16, 128).astype(BF)
        check[s] = pltpu.roll(x[32:40], lax.rem(128 - 16 * z, 128), 1)

    def out_send(s, n):
        g = pl.ds(s, n)
        for d in range(NZ - 1):
            outs[s, d] = send(out_s.at[g, zpos[d]], out_r.at[g, z], o_s.at[s, d], o_r.at[s, d], zpeer[d])
        for i in range(s, s + n):
            out_r[i, z] = out_s[i, z]

    def out_wait(s):
        for d in range(NZ - 1):
            outs[s, d].wait_recv()

    lane = lax.broadcasted_iota(jnp.int32, (16, 128), 1)
    tcopies = {}

    def out_end(s):
        low = jnp.zeros((16, 128), F32)
        high = jnp.zeros((16, 128), F32)
        for k in range(NZ):
            piece = out_r[s, k].astype(F32)
            here = (lane >> 4) == k
            low = jnp.where(here, pltpu.roll(piece, (16 * k) % 128, 1), low)
            high = jnp.where(here, pltpu.roll(piece, (16 * k + 112) % 128, 1), high)
        out_ref[s, :, 0:128] = low
        out_ref[s, :, 128:256] = high
        out_ref[s, :, 256:264] = pltpu.roll(out_r[s, z].astype(F32), 96, 1)[:, 0:8]

    def term_send(which):
        first, count = which[0], len(which)
        solved = out_ref[first : first + count, :, 0:256].reshape(16 * count, 256).astype(BF)
        solved = jnp.concatenate([solved, jnp.zeros((128 - 16 * count, 256), BF)], axis=0)
        term_t[first] = nt(cw_ref[...], solved).reshape(4, 8, 128)
        tcopies[first] = [
            send(term_t.at[first, rpos[d]], got_t.at[first, d], t_s.at[first, d], t_r.at[first, d], rpeer[d])
            for d in range(NR - 1)
        ]

    def term_end(which):
        first = which[0]
        for c in tcopies[first]:
            c.wait_recv()
        total = term_t[first, rhs]
        for d in range(NR - 1):
            total = total + got_t[first, d]
        for i, s in enumerate(which):
            part = total if i == 0 else pltpu.roll(total, 128 - 16 * i, 1)
            gap_ref[s] = (check[s] - part)[:, 0:16]

    rs_in.wait()
    turn(3)
    s_in.wait()
    products(3)
    d_in.wait()
    w_in.wait()
    permute()
    turn(2)
    products(2)
    pl.semaphore_wait(barrier, len(friends))
    phase1_send(3)
    w1_send()
    fac_send(0)
    phase1_send(2)
    turn(1)
    products(1)
    w2_send(0)
    phase2_send(3)
    w2_send(1)
    fac_send(1)
    phase1_send(1)
    turn(0)
    products(0)
    fac_share(0)
    phase3_send(3)
    e_send(0)
    phase2_send(2)
    phase1_send(0)
    fac_share(1)
    phase3_end(3)
    head = gather(rg, 3, rem[3].astype(BF), rg_s, rg_r)
    phase3_send(2)
    fac_end(1)
    e_send(1)
    phase2_send(1)

    done(head)
    x = nt(whole(rg, 3), factor(3, 3))
    copies = gather(xg, 3, x.astype(BF), xg_s, xg_r)
    out_keep(3, x)
    phase3_end(2)
    head = gather(rg, 2, rem[2].astype(BF), rg_s, rg_r)
    e_share(0)
    phase3_send(1)
    phase2_send(0)
    fac_send(2)
    fac_end(0)
    done(head)
    x = nt(whole(rg, 2), factor(2, 2))
    done(copies)
    e_end(0)
    x = x - nt(whole(xg, 3), folded(2, 3))
    copies = gather(xg, 2, x.astype(BF), xg_s, xg_r)
    out_keep(2, x)
    phase3_end(1)
    head = gather(rg, 1, rem[1].astype(BF), rg_s, rg_r)
    phase3_send(0)
    e_share(1)
    fac_share(2)
    done(head)
    e_end(1)
    x = nt(whole(rg, 1), factor(1, 1)) - nt(whole(xg, 3), folded(1, 3))
    done(copies)
    x = x - nt(whole(xg, 2), folded(1, 2))
    copies = gather(xg, 1, x.astype(BF), xg_s, xg_r)
    phase3_end(0)
    fac_end(2)
    rem[0] = rem[0] - nt(whole(xg, 3), factor(0, 3)) - nt(whole(xg, 2), factor(0, 2))
    head = gather(rg, 0, rem[0].astype(BF), rg_s, rg_r)
    out_keep(1, x)
    out_send(1, 3)
    cw_in.wait()
    done(head)
    x = nt(whole(rg, 0), factor(0, 0))
    done(copies)
    x = x - nt(whole(xg, 1), folded(0, 1))
    out_keep(0, x)
    out_send(0, 1)
    out_wait(1)
    out_end(3)
    out_end(2)
    out_end(1)
    term_send((1, 2, 3))
    early = len(sends)
    for c in sends[: early - 10]:
        c.wait_send()
    out_wait(0)
    out_end(0)
    term_send((0,))
    term_end((1, 2, 3))
    term_end((0,))

    for c in sends[early - 10 :]:
        c.wait_send()


def shards(trail_factor, trail_solution, window_factor, diag_inverse, right_side, check_weights):
    vm = pl.BlockSpec(memory_space=pltpu.VMEM)
    hbm = pl.BlockSpec(memory_space=pl.ANY)
    dma = pltpu.SemaphoreType.DMA
    out, gap = pl.pallas_call(
        kernel,
        out_shape=(
            jax.ShapeDtypeStruct((4, 16, 264), F32),
            jax.ShapeDtypeStruct((4, 8, 16), F32),
        ),
        in_specs=[hbm] * 6,
        out_specs=(vm, vm),
        scratch_shapes=[
            pltpu.VMEM((4, 4, 8, 2, 16, 1024), BF),
            pltpu.VMEM((264, 1024), BF),
            pltpu.VMEM((4, 16, 4096), BF),
            pltpu.VMEM((4, 16, 1024), BF),
            pltpu.VMEM((4, 16, 264), F32),
            pltpu.VMEM((32, 256), BF),
            pltpu.VMEM((128, 384), F32),
            pltpu.VMEM((4, 264, 128), F32),
            pltpu.VMEM((3, 2, 8, 16, 1024), BF),
            pltpu.VMEM((2, 2, 8, 16, 128), BF),
            pltpu.VMEM((8, 2, 8, 16, 128), BF),
            pltpu.VMEM((2, 2, 8, 128, 128), BF),
            pltpu.VMEM((4, 4, 2, 9, 16, 128), BF),
            pltpu.VMEM((4, 2, 4, 8, 16, 128), BF),
            pltpu.VMEM((4, 3, 2, 9, 16, 128), BF),
            pltpu.VMEM((4, 4, 8, 16, 128), BF),
            pltpu.VMEM((4, 2, 9, 16, 128), BF),
            pltpu.VMEM((4, 4, 8, 16, 128), BF),
            pltpu.VMEM((4, 9, 16, 128), BF),
            pltpu.VMEM((4, 3, 8, 16, 128), BF),
            pltpu.VMEM((4, 8, 3, 16, 128), BF),
            pltpu.VMEM((4, 7, 3, 16, 128), BF),
            pltpu.VMEM((4, 48, 128), F32),
            pltpu.VMEM((4, 8, 48, 128), BF),
            pltpu.VMEM((4, 8, 48, 128), BF),
            pltpu.VMEM((4, 8, 16, 128), BF),
            pltpu.VMEM((4, 8, 16, 128), BF),
            pltpu.VMEM((4, 8, 128), F32),
            pltpu.VMEM((2, 4, 8, 128), F32),
            pltpu.VMEM((2, 3, 8, 128), F32),
            dma((4, 4)), dma((5,)),
            dma((3, 8)), dma((3, 8)), dma((3,)), dma((3,)),
            dma((7,)), dma((7,)), dma((2, 7)), dma((2, 7)), dma((2, 7)), dma((2, 7)), dma((2,)), dma((2,)),
            dma((4, 3)), dma((4, 3)), dma((4,)), dma((4,)),
            dma((4,)), dma((4,)), dma((4, 3)), dma((4, 3)),
            dma((4, 7)), dma((4, 7)),
            dma((4, 7)), dma((4, 7)), dma((4, 7)), dma((4, 7)),
            dma((4, 7)), dma((4, 7)),
            dma((2, 3)), dma((2, 3)),
        ],
        compiler_params=pltpu.CompilerParams(
            collective_id=0, has_side_effects=True, vmem_limit_bytes=60 * 2**20
        ),
    )(
        trail_factor.reshape(4, 4, 8, 2, 16, 1024),
        trail_solution.T,
        window_factor,
        diag_inverse,
        right_side,
        check_weights[0].T,
    )
    return out, gap.transpose(0, 2, 1)


def solution(mesh):
    in_specs = (
        P(None, "col"),
        P("col", "rhs"),
        P(None, "col", None),
        P(None, "col", None),
        P(None, "col", "rhs"),
        P("rhs", None, None),
    )
    out_specs = (P(None, "col", "rhs"), P(None, "col", "rhs"))
    return jax.shard_map(shards, mesh=mesh, in_specs=in_specs, out_specs=out_specs, check_vma=False)
```

```python
import functools

import jax
import jax.numpy as jnp
from jax import lax
from jax.experimental import pallas as pl
from jax.experimental.pallas import tpu as pltpu
from jax.sharding import PartitionSpec as P

MESH = pl.DeviceIdType.MESH
BF = jnp.bfloat16
F32 = jnp.float32
NY, NZ, NX, NR = 4, 8, 2, 4
WIN = 4
KEPT = [(2, 2), (1, 1), (3, 3), (0, 0), (0, 2), (0, 3)]
SLOT = {pair: i for i, pair in enumerate(KEPT)}
FOLDED = [(2, 3), (1, 2), (0, 1), (1, 3)]
FOLD = {pair: i for i, pair in enumerate(FOLDED)}


def nt(a, b):
    return lax.dot_general(a, b, (((1,), (1,)), ((), ())), preferred_element_type=F32)


def kernel(
    f_hbm, s_hbm, w_hbm, d_hbm, rs_hbm, cw_hbm, out_ref, gap_ref,
    fv, st, w_ref, d_ref, rs_ref, cw_ref, rs_pad, rs_t, fac, ws, wfull, efac,
    acc_b, acc_c, got_b1, got_c1, red_b, red_c, got_b2, got_c2, red, got3,
    rem, rg, xg, out_s, out_r, check, term_t, got_t,
    f_sem, in_sem, fac_ss, fac_rs, fac_cs, fac_cr, w1_s, w1_r, w2_s, w2_r, e_s, e_r, ec_s, ec_r,
    b1_s, b1_r, c1_s, c1_r, b2_s, b2_r, c2_s, c2_r, z_s, z_r,
    rg_s, rg_r, xg_s, xg_r, o_s, o_r, t_s, t_r,
):
    col = lax.axis_index("col")
    rhs = lax.axis_index("rhs")
    y = lax.div(col, NZ * NX)
    z = lax.rem(lax.div(col, NX), NZ)
    xh = lax.rem(col, NX)
    core = lax.rem(rhs, 2)
    mine = y * NX + xh

    def at(yy, zz, xx):
        return ((yy * NZ + zz) * NX + xx, rhs)

    ypeer = [at(lax.rem(y + d, NY), z, xh) for d in range(1, NY)]
    ypos = [lax.rem(y + d, NY) for d in range(1, NY)]
    xpeer = at(y, z, 1 - xh)
    zpos = [lax.rem(z + d, NZ) for d in (4, 3, 5, 2, 6, 1, 7)]
    zpeer = [at(y, p, xh) for p in zpos]
    yxpeer = [at(lax.rem(y + d, NY), z, 1 - xh) for d in (2, 1, 3)] + [xpeer, ypeer[1], ypeer[0], ypeer[2]]
    sibling = (col, rhs + 1 - 2 * core)
    rpeer = [(col, lax.rem(rhs + d, NR)) for d in range(1, NR)]
    rpos = [lax.rem(rhs + d, NR) for d in range(1, NR)]

    sends = []

    def send(src, dst, ss, rs, to):
        c = pltpu.make_async_remote_copy(
            src_ref=src, dst_ref=dst, send_sem=ss, recv_sem=rs, device_id=to, device_id_type=MESH
        )
        c.start()
        sends.append(c)
        return c

    barrier = pltpu.get_barrier_semaphore()
    friends = yxpeer + zpeer + rpeer
    for who in friends:
        pl.semaphore_signal(barrier, inc=1, device_id=who, device_id_type=MESH)

    def done(copies):
        for c in copies:
            c.wait_recv()

    s_in = pltpu.make_async_copy(s_hbm, st, in_sem.at[0])
    rs_in = pltpu.make_async_copy(rs_hbm, rs_ref, in_sem.at[1])
    d_in = pltpu.make_async_copy(d_hbm, d_ref, in_sem.at[2])
    w_in = pltpu.make_async_copy(w_hbm, w_ref, in_sem.at[3])
    cw_in = pltpu.make_async_copy(cw_hbm, cw_ref, in_sem.at[4])

    def f_start(s):
        for yy in range(NY):
            pltpu.make_async_copy(f_hbm.at[s, yy], fv.at[s, yy], f_sem.at[s, yy]).start()

    rs_in.start()
    s_in.start()
    f_start(3)
    d_in.start()
    w_in.start()
    for s in range(WIN - 2, -1, -1):
        f_start(s)
    cw_in.start()

    def permute():
        n = lax.broadcasted_iota(jnp.int32, (256, 256), 0)
        m = lax.broadcasted_iota(jnp.int32, (256, 256), 1)
        natural = ((m >> 4) & 7) * 32 + (m >> 7) * 16 + (m & 15)
        perm = jnp.where(n == natural, 1.0, 0.0).astype(BF)
        for g in range(NY):
            rows = []
            for r, c in KEPT + FOLDED:
                if r == c:
                    rows.append(d_ref[r, :, g * 256 : (g + 1) * 256])
                else:
                    rows.append(w_ref[r, :, c * 1024 + g * 256 : c * 1024 + (g + 1) * 256])
            moved = jnp.dot(jnp.concatenate(rows, axis=0), perm, preferred_element_type=F32).astype(BF)
            moved = moved.reshape(10, 16, 256)
            for a in range(3):
                fac[a, core, z, :, g * 256 : (g + 1) * 256] = jnp.where(core == 0, moved[2 * a], moved[2 * a + 1])
            for i in range(4):
                for x in range(NX):
                    ws[i // 2, i % 2, g * NX + x] = moved[6 + i, :, x * 128 : (x + 1) * 128]

    fac_c, fac_shared, e_c, e_shared, w1, w2 = {}, {}, {}, {}, [], {}

    def fac_send(a):
        part = fac.at[a, core, z]
        fac_c[a] = [send(part, part, fac_ss.at[a, d], fac_rs.at[a, d], zpeer[d]) for d in range(NZ - 1)]

    def ring_send(a, direction, step, zz):
        part = fac.at[a, core, zz]
        to = zpeer[-1] if direction else zpeer[0]
        slot = 4 * direction + step
        return send(part, part, fac_ss.at[a, slot], fac_rs.at[a, slot], to)

    ups, downs = {}, {}

    def ring_start(a):
        ups[a] = [ring_send(a, 0, 0, z)]
        downs[a] = [ring_send(a, 1, 0, z)]
        fac_c[a] = []

    def ring_step(a, step):
        ups[a][step].wait_recv()
        if step < 3:
            ups[a].append(ring_send(a, 0, step + 1, lax.rem(z + NZ - 1 - step, NZ)))
            downs[a][step].wait_recv()
            if step < 2:
                downs[a].append(ring_send(a, 1, step + 1, lax.rem(z + 1 + step, NZ)))

    def fac_share(a):
        done(fac_c[a])
        fac_shared[a] = send(fac.at[a, core], fac.at[a, core], fac_cs.at[a], fac_cr.at[a], sibling)

    def fac_end(a):
        fac_shared[a].wait_recv()

    def w1_send():
        wfull[mine, :, z] = ws[:, core, z]
        for d in range(NZ - 1):
            w1.append(send(ws.at[:, core, zpos[d]], wfull.at[mine, :, z], w1_s.at[d], w1_r.at[d], zpeer[d]))

    def w2_send(i):
        if i == 0:
            done(w1)
        part = wfull.at[mine, i]
        w2[i] = [send(part, part, w2_s.at[i, d], w2_r.at[i, d], who) for d, who in enumerate(yxpeer)]

    def e_send(i):
        done(w2[i])
        inverse = (fac[0, core] if i == 0 else fac[1 - core, 1]).reshape(128, 1024)
        block = jnp.concatenate([wfull[p, i].reshape(128, 128) for p in range(NY * NX)], axis=0)
        efac[i, core, z] = jnp.dot(inverse, block, preferred_element_type=F32).astype(BF)
        part = efac.at[i, core, z]
        e_c[i] = [send(part, part, e_s.at[i, d], e_r.at[i, d], zpeer[d]) for d in range(NZ - 1)]

    def e_share(i):
        done(e_c[i])
        e_shared[i] = send(efac.at[i, core], efac.at[i, core], ec_s.at[i], ec_r.at[i], sibling)

    def e_end(i):
        e_shared[i].wait_recv()

    def folded(r, c):
        i = FOLD[r, c]
        return jnp.concatenate([efac[i // 2, i % 2, k] for k in range(NZ)], axis=1)

    def turn(s):
        rs_pad[...] = jnp.zeros_like(rs_pad)
        rs_pad[pl.ds(pl.multiple_of(z * 16, 16), 16), 0:264] = rs_ref[s]
        for c in range(3):
            t = rs_pad[:, c * 128 : (c + 1) * 128].T
            if c < 2:
                rs_t[s, c * 128 : (c + 1) * 128] = t
            else:
                rs_t[s, 256:264] = t[0:8]

    def products(s):
        def one(yy, _):
            pltpu.make_async_copy(f_hbm.at[s, yy], fv.at[s, yy], f_sem.at[s, yy]).wait()
            here = jnp.where(yy == y, 1.0, 0.0).astype(F32)
            block = jnp.concatenate(
                [fv[s, yy, :, x].reshape(128, 1024) for x in range(NX)], axis=0
            )
            both = nt(st[...], block)
            for x in range(NX):
                scale = here * jnp.where(xh == x, 1.0, 0.0).astype(F32)
                value = scale * rs_t[s] - both[:, x * 128 : (x + 1) * 128]
                value = jnp.concatenate([value, jnp.zeros((8, 128), F32)], axis=0).astype(BF)
                acc_b[s, yy, x, 0:8] = value[0:128].reshape(8, 16, 128)
                acc_b[s, yy, x, 8:9] = value[256:272].reshape(1, 16, 128)
                acc_c[s, x, yy] = value[128:256].reshape(8, 16, 128)
            return 0

        lax.fori_loop(0, NY, one, 0)

    b1, c1, b2, c2, zz_c = {}, {}, {}, {}, {}

    def phase1_send(s, n=1):
        g = pl.ds(s, n)
        for d in range(NY - 1):
            b1[s, d] = send(acc_b.at[g, ypos[d]], got_b1.at[g, d], b1_s.at[s, d], b1_r.at[s, d], ypeer[d])
        c1[s] = send(acc_c.at[g, 1 - xh], got_c1.at[g], c1_s.at[s], c1_r.at[s], xpeer)

    def phase2_send(s, n=1):
        g = pl.ds(s, n)
        for d in range(NY - 1):
            b1[s, d].wait_recv()
        total = acc_b[g, y].astype(F32)
        for d in range(NY - 1):
            total = total + got_b1[g, d].astype(F32)
        red_b[g] = total.astype(BF)
        b2[s] = send(red_b.at[g, 1 - xh], got_b2.at[g], b2_s.at[s], b2_r.at[s], xpeer)
        c1[s].wait_recv()
        red_c[g] = (acc_c[g, xh].astype(F32) + got_c1[g].astype(F32)).astype(BF)
        for d in range(NY - 1):
            c2[s, d] = send(red_c.at[g, ypos[d]], got_c2.at[g, d], c2_s.at[s, d], c2_r.at[s, d], ypeer[d])

    def phase3_send(s, n=1):
        g = pl.ds(s, n)
        b2[s].wait_recv()
        total = (red_b[g, xh].astype(F32) + got_b2[g].astype(F32)).astype(BF)
        for i in range(n):
            red[s + i, :, 0:1] = total[i, 0:8].reshape(8, 1, 16, 128)
            for k in range(NZ):
                red[s + i, k, 2:3] = total[i, 8:9]
        for d in range(NY - 1):
            c2[s, d].wait_recv()
        total = red_c[g, y].astype(F32)
        for d in range(NY - 1):
            total = total + got_c2[g, d].astype(F32)
        total = total.astype(BF)
        for i in range(n):
            red[s + i, :, 1:2] = total[i].reshape(8, 1, 16, 128)
        for d in range(NZ - 1):
            zz_c[s, d] = send(red.at[g, zpos[d]], got3.at[g, d], z_s.at[s, d], z_r.at[s, d], zpeer[d])

    def phase3_end(s, n=1):
        for d in range(NZ - 1):
            zz_c[s, d].wait_recv()
        for i in range(s, s + n):
            total = red[i, z].astype(F32)
            for d in range(NZ - 1):
                total = total + got3[i, d].astype(F32)
            rem[i] = total.reshape(48, 128)

    def gather(buf, s, value, ss, rs):
        buf[s, mine] = value
        return [
            send(buf.at[s, mine], buf.at[s, mine], ss.at[s, d], rs.at[s, d], who)
            for d, who in enumerate(yxpeer)
        ]

    def whole(buf, s):
        return jnp.concatenate([buf[s, p] for p in range(NY * NX)], axis=1)

    def factor(r, c):
        i = SLOT[r, c]
        return fac[i // 2, i % 2].reshape(128, 1024)

    outs = {}

    def out_keep(s, x):
        full = jnp.concatenate([x, jnp.zeros((80, 128), F32)], axis=0).T
        out_s[s] = full.reshape(8, 16, 128).astype(BF)
        check[s] = pltpu.roll(x[32:40], lax.rem(128 - 16 * z, 128), 1)

    def out_send(s, n):
        g = pl.ds(s, n)
        for d in range(NZ - 1):
            outs[s, d] = send(out_s.at[g, zpos[d]], out_r.at[g, z], o_s.at[s, d], o_r.at[s, d], zpeer[d])
        for i in range(s, s + n):
            out_r[i, z] = out_s[i, z]

    def out_wait(s):
        for d in range(NZ - 1):
            outs[s, d].wait_recv()

    lane = lax.broadcasted_iota(jnp.int32, (16, 128), 1)
    tcopies = {}

    def out_end(s):
        low = jnp.zeros((16, 128), F32)
        high = jnp.zeros((16, 128), F32)
        for k in range(NZ):
            piece = out_r[s, k].astype(F32)
            here = (lane >> 4) == k
            low = jnp.where(here, pltpu.roll(piece, (16 * k) % 128, 1), low)
            high = jnp.where(here, pltpu.roll(piece, (16 * k + 112) % 128, 1), high)
        out_ref[s, :, 0:128] = low
        out_ref[s, :, 128:256] = high
        out_ref[s, :, 256:264] = pltpu.roll(out_r[s, z].astype(F32), 96, 1)[:, 0:8]

    def term_send(which):
        first, count = which[0], len(which)
        solved = out_ref[first : first + count, :, 0:256].reshape(16 * count, 256).astype(BF)
        solved = jnp.concatenate([solved, jnp.zeros((128 - 16 * count, 256), BF)], axis=0)
        term_t[first] = nt(cw_ref[...], solved).reshape(4, 8, 128)
        tcopies[first] = [
            send(term_t.at[first, rpos[d]], got_t.at[first, d], t_s.at[first, d], t_r.at[first, d], rpeer[d])
            for d in range(NR - 1)
        ]

    def term_end(which):
        first = which[0]
        for c in tcopies[first]:
            c.wait_recv()
        total = term_t[first, rhs]
        for d in range(NR - 1):
            total = total + got_t[first, d]
        for i, s in enumerate(which):
            part = total if i == 0 else pltpu.roll(total, 128 - 16 * i, 1)
            gap_ref[s] = (check[s] - part)[:, 0:16]

    rs_in.wait()
    turn(3)
    s_in.wait()
    products(3)
    d_in.wait()
    w_in.wait()
    permute()
    turn(2)
    products(2)
    pl.semaphore_wait(barrier, len(friends))
    phase1_send(3)
    w1_send()
    fac_send(0)
    phase1_send(2)
    turn(1)
    products(1)
    w2_send(0)
    phase2_send(3)
    w2_send(1)
    fac_send(1)
    phase1_send(1)
    turn(0)
    products(0)
    fac_share(0)
    phase3_send(3)
    e_send(0)
    phase2_send(2)
    phase1_send(0)
    fac_share(1)
    phase3_end(3)
    head = gather(rg, 3, rem[3].astype(BF), rg_s, rg_r)
    phase3_send(2)
    fac_end(1)
    e_send(1)
    phase2_send(1)

    done(head)
    x = nt(whole(rg, 3), factor(3, 3))
    copies = gather(xg, 3, x.astype(BF), xg_s, xg_r)
    out_keep(3, x)
    phase3_end(2)
    head = gather(rg, 2, rem[2].astype(BF), rg_s, rg_r)
    e_share(0)
    phase3_send(1)
    phase2_send(0)
    fac_send(2)
    fac_end(0)
    done(head)
    x = nt(whole(rg, 2), factor(2, 2))
    done(copies)
    e_end(0)
    x = x - nt(whole(xg, 3), folded(2, 3))
    copies = gather(xg, 2, x.astype(BF), xg_s, xg_r)
    out_keep(2, x)
    phase3_end(1)
    head = gather(rg, 1, rem[1].astype(BF), rg_s, rg_r)
    phase3_send(0)
    e_share(1)
    fac_share(2)
    done(head)
    e_end(1)
    x = nt(whole(rg, 1), factor(1, 1)) - nt(whole(xg, 3), folded(1, 3))
    done(copies)
    x = x - nt(whole(xg, 2), folded(1, 2))
    copies = gather(xg, 1, x.astype(BF), xg_s, xg_r)
    phase3_end(0)
    fac_end(2)
    rem[0] = rem[0] - nt(whole(xg, 3), factor(0, 3)) - nt(whole(xg, 2), factor(0, 2))
    head = gather(rg, 0, rem[0].astype(BF), rg_s, rg_r)
    out_keep(1, x)
    out_send(1, 3)
    cw_in.wait()
    done(head)
    x = nt(whole(rg, 0), factor(0, 0))
    done(copies)
    x = x - nt(whole(xg, 1), folded(0, 1))
    out_keep(0, x)
    out_send(0, 1)
    out_wait(1)
    out_end(3)
    out_end(2)
    out_end(1)
    term_send((1, 2, 3))
    early = len(sends)
    for c in sends[: early - 10]:
        c.wait_send()
    out_wait(0)
    out_end(0)
    term_send((0,))
    term_end((1, 2, 3))
    term_end((0,))

    for c in sends[early - 10 :]:
        c.wait_send()


def shards(trail_factor, trail_solution, window_factor, diag_inverse, right_side, check_weights):
    vm = pl.BlockSpec(memory_space=pltpu.VMEM)
    hbm = pl.BlockSpec(memory_space=pl.ANY)
    dma = pltpu.SemaphoreType.DMA
    out, gap = pl.pallas_call(
        kernel,
        out_shape=(
            jax.ShapeDtypeStruct((4, 16, 264), F32),
            jax.ShapeDtypeStruct((4, 8, 16), F32),
        ),
        in_specs=[hbm] * 6,
        out_specs=(vm, vm),
        scratch_shapes=[
            pltpu.VMEM((4, 4, 8, 2, 16, 1024), BF),
            pltpu.VMEM((264, 1024), BF),
            pltpu.VMEM((4, 16, 4096), BF),
            pltpu.VMEM((4, 16, 1024), BF),
            pltpu.VMEM((4, 16, 264), F32),
            pltpu.VMEM((32, 256), BF),
            pltpu.VMEM((128, 384), F32),
            pltpu.VMEM((4, 264, 128), F32),
            pltpu.VMEM((3, 2, 8, 16, 1024), BF),
            pltpu.VMEM((2, 2, 8, 16, 128), BF),
            pltpu.VMEM((8, 2, 8, 16, 128), BF),
            pltpu.VMEM((2, 2, 8, 128, 128), BF),
            pltpu.VMEM((4, 4, 2, 9, 16, 128), BF),
            pltpu.VMEM((4, 2, 4, 8, 16, 128), BF),
            pltpu.VMEM((4, 3, 2, 9, 16, 128), BF),
            pltpu.VMEM((4, 4, 8, 16, 128), BF),
            pltpu.VMEM((4, 2, 9, 16, 128), BF),
            pltpu.VMEM((4, 4, 8, 16, 128), BF),
            pltpu.VMEM((4, 9, 16, 128), BF),
            pltpu.VMEM((4, 3, 8, 16, 128), BF),
            pltpu.VMEM((4, 8, 3, 16, 128), BF),
            pltpu.VMEM((4, 7, 3, 16, 128), BF),
            pltpu.VMEM((4, 48, 128), F32),
            pltpu.VMEM((4, 8, 48, 128), BF),
            pltpu.VMEM((4, 8, 48, 128), BF),
            pltpu.VMEM((4, 8, 16, 128), BF),
            pltpu.VMEM((4, 8, 16, 128), BF),
            pltpu.VMEM((4, 8, 128), F32),
            pltpu.VMEM((2, 4, 8, 128), F32),
            pltpu.VMEM((2, 3, 8, 128), F32),
            dma((4, 4)), dma((5,)),
            dma((3, 8)), dma((3, 8)), dma((3,)), dma((3,)),
            dma((7,)), dma((7,)), dma((2, 7)), dma((2, 7)), dma((2, 7)), dma((2, 7)), dma((2,)), dma((2,)),
            dma((4, 3)), dma((4, 3)), dma((4,)), dma((4,)),
            dma((4,)), dma((4,)), dma((4, 3)), dma((4, 3)),
            dma((4, 7)), dma((4, 7)),
            dma((4, 7)), dma((4, 7)), dma((4, 7)), dma((4, 7)),
            dma((4, 7)), dma((4, 7)),
            dma((2, 3)), dma((2, 3)),
        ],
        compiler_params=pltpu.CompilerParams(
            collective_id=0, has_side_effects=True, vmem_limit_bytes=60 * 2**20
        ),
    )(
        trail_factor.reshape(4, 4, 8, 2, 16, 1024),
        trail_solution.T,
        window_factor,
        diag_inverse,
        right_side,
        check_weights[0].T,
    )
    return out, gap.transpose(0, 2, 1)


def solution(mesh):
    in_specs = (
        P(None, "col"),
        P("col", "rhs"),
        P(None, "col", None),
        P(None, "col", None),
        P(None, "col", "rhs"),
        P("rhs", None, None),
    )
    out_specs = (P(None, "col", "rhs"), P(None, "col", "rhs"))
    return jax.shard_map(shards, mesh=mesh, in_specs=in_specs, out_specs=out_specs, check_vma=False)
```
